256 devices in a mesh: node: 8 (over y, core), local: 32 (over z, x).
Axes of the slice: x: 4, y: 4, z: 8, core: 2. Of those that a mesh axis runs over, the one named last changes fastest.
Arguments:
- grad_out: bfloat16 [32768, 3584], P(('node', 'local')), may hold values from -24 to 24
- expert_ids: int32 [32768, 8], P(('node', 'local')), may hold values from 0 to 127, as said below
- gate_probs: bfloat16 [32768, 8], P(('node', 'local')), may hold values from 0.099609375 to 1
- down_weight: bfloat16 [131072, 3584], P(('node', 'local')), may hold values from -0.046875 to 0.046875
- hidden_act: bfloat16 [2048, 131072], P(None, ('node', 'local')), may hold values from -32 to 32
Outputs:
- clipped_grad: bfloat16 [131072, 3584], P(('node', 'local'))
- hidden_grad: bfloat16 [2048, 131072], P(None, ('node', 'local'))
- router_grad: float32 [32768, 8], P(('node', 'local'))
The draws below stay inside these ranges and needn't reach their ends.
Inputs may be any that keep to these rules, and one draw needn't show every extreme that they name: `expert_ids`: each token names 8 different experts, two in each of 4 different groups, where expert e lies in group e // 16; each aligned block of 128 tokens names every expert exactly 8 times, so every expert has exactly 2048 rows.
All inputs are finite; a program needn't handle non-finite values.
Results may differ from the reference program's by a relative error of at most 0.0049.
Values may be sent and summed in bfloat16 or wider, within the bound.
A program may use at most 128 MiB of HBM per device.

```python
import math
import jax
import jax.numpy as jnp
from jax import lax

D = 3584
FF = 1024
TOP = 8
GROUPS = 4
TOK_DEV = 128
GROUP_EXPERTS = 16
EXPERTS = 128
SOURCES = 256
TOKENS = 32768
PER_SOURCE = 8
SLOTS = 2048


def draw_grad_out(key, part):
    key = jax.random.fold_in(key, 12)
    key_base, key_cols = jax.random.split(key, 2)
    col_scale = jnp.exp(jax.random.uniform(key_cols, (D,), jnp.float32, jnp.log(0.3), jnp.log(3.0)))
    base_vals = jnp.clip(jax.random.normal(key_base, (TOKENS, D), jnp.float32), -6.0, 6.0)
    values = base_vals * col_scale[None, :]
    return values.astype(jnp.bfloat16)


def draw_hidden_act(key, part):
    key = jax.random.fold_in(key, 11)
    key_base, key_cols = jax.random.split(key, 2)
    columns = EXPERTS * FF
    col_scale = jnp.exp(jax.random.uniform(key_cols, (columns,), jnp.float32, jnp.log(0.3), jnp.log(3.0)))
    expert_pos = (jnp.arange(columns) // FF).astype(jnp.float32) / max(EXPERTS - 1, 1)
    expert_scale = jnp.power(3.0, expert_pos)
    base_vals = jnp.clip(jax.random.normal(key_base, (SLOTS, columns), jnp.float32), -6.0, 6.0)
    values = 0.5 * base_vals * col_scale[None, :] * expert_scale[None, :]
    return jnp.clip(values, -32.0, 32.0).astype(jnp.bfloat16)


def draw_expert_ids(key, part):
    key = jax.random.fold_in(key, 13)
    node_count = EXPERTS // GROUP_EXPERTS
    half_count = GROUP_EXPERTS // 2
    blocks = TOK_DEV // node_count
    key_shift, key_pick, key_order = jax.random.split(key, 3)
    shifts = jax.random.randint(key_shift, (SOURCES, blocks), 0, node_count)
    pick_keys = jax.random.split(key_pick, SOURCES * blocks)
    picked = jax.vmap(lambda sub_key: jax.random.permutation(sub_key, node_count))(pick_keys)
    picked = picked[:, :GROUPS].reshape(SOURCES, blocks, GROUPS)
    order_keys = jax.random.split(key_order, SOURCES * node_count)
    orders = jax.vmap(lambda sub_key: jax.random.permutation(sub_key, GROUP_EXPERTS))(order_keys)
    orders = orders.reshape(SOURCES, node_count, GROUP_EXPERTS)
    within = jnp.arange(node_count)
    start_node = (within[None, None, :] + shifts[:, :, None]) % node_count
    chosen = (start_node[..., None] + picked[:, :, None, :]) % node_count
    lane_index = (jnp.arange(blocks)[:, None] * GROUPS + jnp.arange(GROUPS)[None, :]) % half_count
    source_ids = jnp.arange(SOURCES)[:, None, None, None]
    first_pick = orders[source_ids, chosen, lane_index[None, :, None, :]]
    second_pick = orders[source_ids, chosen, lane_index[None, :, None, :] + half_count]
    paired = jnp.stack([first_pick, second_pick], axis=-1) + chosen[..., None] * GROUP_EXPERTS
    return paired.reshape(SOURCES * TOK_DEV, TOP).astype(jnp.int32)


def level_of(rng, shape, shards, low, top_value):
    def one(axis_at, shards_of):
        heights = jax.random.uniform(jax.random.fold_in(jax.random.fold_in(rng, 6), axis_at), (shards_of,), jnp.float32, low / len(shards), top_value / len(shards))
        return jnp.repeat(jnp.exp(heights), shape[axis_at] // shards_of).reshape((-1,) + (1,) * (len(shape) - axis_at - 1))

    level = one(*shards[0])
    for cut in shards[1:]:
        level = level * one(*cut)
    return level


def centred(key, shape, spread, bound, shards=(), kind=jnp.bfloat16):
    level = level_of(key, shape, shards, -0.22, 0.18) if shards else 1.0
    entries = jax.random.normal(key, shape, jnp.float32) * spread * level
    return jnp.minimum(jnp.maximum(entries, -bound), bound).astype(kind)


def setup_inputs(seed: int = 0) -> dict:
    splits = jax.random.split(jax.random.key(seed), 6)
    grad_out = draw_grad_out(jax.random.fold_in(splits[5], 71), 0)
    expert_ids = draw_expert_ids(jax.random.fold_in(splits[5], 71), 0)
    gate_probs = jnp.clip(jnp.exp(math.log(1.0) - 2.306499 * jax.random.uniform(splits[2], (TOKENS, TOP), jnp.float32) ** level_of(splits[2], (TOKENS, TOP), ((0, 256),), -0.2, 0.2)), 0.099609375, 1.0).astype(jnp.bfloat16)
    down_weight = centred(splits[3], (EXPERTS * FF, D), (16 * FF) ** -0.5, 0.046875, ((0, 256),))
    hidden_act = draw_hidden_act(jax.random.fold_in(splits[5], 71), 0)
    return dict(grad_out=grad_out, expert_ids=expert_ids, gate_probs=gate_probs, down_weight=down_weight, hidden_act=hidden_act)


clip_rms = 0.25
square_eps = 1e-06

def reference(grad_out, expert_ids, gate_probs, down_weight, hidden_act):
    routes_dev = TOK_DEV * TOP
    flat_ids = expert_ids.reshape(SOURCES, routes_dev)
    expert_range = jnp.arange(EXPERTS, dtype=jnp.int32)
    onehot = (flat_ids[:, :, None] == expert_range[None, None, :]).astype(jnp.int32)
    rank_of = lax.optimization_barrier(jnp.sum(jnp.cumsum(onehot, axis=1) * onehot, axis=2)) - 1
    source_ids = jnp.arange(SOURCES, dtype=jnp.int32)[:, None]
    slot_of = (source_ids * PER_SOURCE + rank_of).astype(jnp.int32)
    route_ids = jnp.arange(TOKENS * TOP, dtype=jnp.int32).reshape(SOURCES, routes_dev)
    slot_table = jnp.zeros((EXPERTS, SLOTS), jnp.int32).at[flat_ids, slot_of].set(route_ids)
    flat_gates = gate_probs.reshape(TOKENS * TOP)

    def one_expert(expert_index):
        routes = slot_table[expert_index]
        row_data = grad_out[routes // TOP]
        gate_wide = flat_gates[routes].astype(jnp.float32)[:, None]
        weight = lax.dynamic_slice_in_dim(down_weight, expert_index * FF, FF, 0)
        activations = lax.dynamic_slice_in_dim(hidden_act, expert_index * FF, FF, 1)
        project = lax.dot_general(row_data, weight, (((1,), (1,)), ((), ())), preferred_element_type=jnp.float32)
        hidden_part = (gate_wide * project).astype(jnp.bfloat16)
        partial_value = lax.optimization_barrier(jnp.sum(activations.astype(jnp.float32) * project, axis=1))
        scaled = (gate_wide * activations.astype(jnp.float32)).astype(jnp.bfloat16)
        weight_grad = lax.dot_general(scaled, row_data, (((0,), (0,)), ((), ())), preferred_element_type=jnp.float32)
        return (weight_grad, hidden_part, partial_value, jnp.sum(weight_grad * weight_grad))
    weight_grads, hidden_parts, partials, squares = lax.map(one_expert, expert_range)
    total_sq = jnp.sum(squares)
    factor = clip_rms / jnp.sqrt(total_sq / jnp.float32(EXPERTS * FF * D) + square_eps)
    clipped = (weight_grads * factor).astype(jnp.bfloat16).reshape(EXPERTS * FF, D)
    hidden_grad = jnp.transpose(hidden_parts, (1, 0, 2)).reshape(SLOTS, EXPERTS * FF)
    router_flat = jnp.zeros((TOKENS * TOP,), jnp.float32).at[slot_table.reshape(-1)].set(partials.reshape(-1))
    return (clipped, hidden_grad, router_flat.reshape(TOKENS, TOP))
```

```python
import jax
import jax.numpy as jnp
from jax import lax
from jax.experimental import pallas as pl
from jax.experimental.pallas import tpu as pltpu
from jax.sharding import PartitionSpec as P

MESH = pl.DeviceIdType.MESH
F32 = jnp.float32
BF16 = jnp.bfloat16

D = 3584
FFH = 512
TOK = 128
SLOTS = 2048
ENTRIES = 469762048
CLIP = 0.25
EPS = 1e-06

CG = 1280
CA = D - CG
TW = D + CG
HALF = TW // 2
NB = 4
NZ = 8
CT = 256


def nt(a, b):
    return lax.dot_general(a, b, (((1,), (1,)), ((), ())), preferred_element_type=F32)


def step_z(z, k):
    return lax.rem(z + ((k + 1) // 2) * (1 - 2 * lax.rem(k, 2)) + NZ, NZ)


def kernel(
    tok_hbm, ids_ref, gate_ref, w_hbm, act_hbm,
    out_hbm, hg_hbm, router_ref,
    tx, rows, stage, wv, actv, hgv, wg, sel, meta, gvb, gvr, proj, sct, gate_s, rk_s,
    pv, a1, b1, a2, b2, a3, b3, a4, b4,
    in_sem, out_sem, meta_s, meta_r, zmeta_s, zmeta_r, pc_s, pc_r, zr_s, zr_r, sib_s, sib_r,
    fh_s, fh_r, fw_s, fw_r, gv_s, gv_r, e1_s, e1_r, e2_s, e2_r, e3_s, e3_r, e4_s, e4_r,
):
    node = lax.axis_index("node")
    local = lax.axis_index("local")
    y, c = node // 2, lax.rem(node, 2)
    z, x = local // 4, lax.rem(local, 4)
    xp = lax.rem(x, 2)
    pair = x // 2
    qx = lax.rem(xp + pair, 2)
    x_partner = x + 1 - 2 * xp
    me8 = pair * 4 + y

    def dev(xx, yy, zz, cc):
        return (2 * yy + cc, 4 * zz + xx)

    partner = dev(x_partner, y, z, c)
    sibling = dev(x, y, z, 1 - c)
    diagonal = dev(x_partner, y, z, 1 - c)

    def entry_x(p):
        return qx + p * (3 - 2 * qx)

    def remote(src, dst, ss, rs, to):
        return pltpu.make_async_remote_copy(
            src_ref=src, dst_ref=dst, send_sem=ss, recv_sem=rs, device_id=to, device_id_type=MESH
        )

    def landed(dst, rs):
        pltpu.make_async_copy(dst, dst, rs).wait()

    def zpeer(d):
        return dev(x, y, lax.rem(z + d + NZ, NZ), c)

    own_rows = pl.ds(pl.multiple_of(c * TOK, TOK), TOK)
    sib_rows = pl.ds(pl.multiple_of((1 - c) * TOK, TOK), TOK)
    tok_copy = pltpu.make_async_copy(tok_hbm, tx.at[z, own_rows, pl.ds(0, D)], in_sem.at[0])
    tok_copy.start()
    act_copy = pltpu.make_async_copy(act_hbm, actv, in_sem.at[1])
    w_copy = pltpu.make_async_copy(w_hbm, wv, in_sem.at[2])
    mine = xp * 2 + c
    meta[z, mine, 0:8, :] = ids_ref[...].astype(F32)
    meta[z, mine, 8:16, :] = gate_ref[...].astype(F32)

    barrier = pltpu.get_barrier_semaphore()

    def greet(to):
        pl.semaphore_signal(barrier, inc=1, device_id=to, device_id_type=MESH)

    for to in (partner, sibling, diagonal):
        greet(to)
    for d in range(1, NZ):
        greet(zpeer(d))
    for m in range(8):
        @pl.when(m != me8)
        def _(m=m):
            greet(dev(entry_x(m // 4), m % 4, z, c))
    pl.semaphore_wait(barrier, 3 + 7 + 7)

    others = ((partner, (1 - xp) * 2 + c), (sibling, xp * 2 + 1 - c), (diagonal, (1 - xp) * 2 + 1 - c))
    meta_copies = [
        remote(meta.at[z, mine], meta.at[z, mine], meta_s.at[j], meta_r.at[j], to)
        for j, (to, _) in enumerate(others)
    ]
    for cp in meta_copies:
        cp.start()
    tok_copy.wait()
    part_cols = (pl.ds(0, D), pl.ds(D, CG))
    pre = remote(
        tx.at[z, own_rows, pl.ds(CA, CG)], tx.at[z, own_rows, pl.ds(D, CG)], pc_s, pc_r, partner
    )
    pre.start()

    def zsend(zs, cols, ss, rs, d):
        return remote(tx.at[zs, own_rows, cols], tx.at[zs, own_rows, cols], ss, rs, zpeer(d))

    def sib_copy(zs, k, part):
        ref = tx.at[zs, own_rows, part_cols[part]]
        return remote(ref, ref, sib_s.at[k, part], sib_r.at[k, part], sibling)

    def own_send(part):
        zsend(z, part_cols[part], zr_s.at[0, part], zr_r.at[1, part], 1).start()
        zsend(z, part_cols[part], zr_s.at[7, part], zr_r.at[2, part], -1).start()
        sib_copy(z, 0, part).start()

    own_send(0)
    for j, (_, slot) in enumerate(others):
        landed(meta.at[z, slot], meta_r.at[j])
    zmeta = [
        remote(meta.at[z], meta.at[z], zmeta_s.at[d], zmeta_r.at[d], zpeer(d)) for d in range(1, NZ)
    ]
    for cp in zmeta:
        cp.start()
    act_copy.start()
    w_copy.start()
    pre.wait_recv()
    own_send(1)
    for d in range(1, NZ):
        landed(meta.at[lax.rem(z - d + NZ, NZ)], zmeta_r.at[d])

    row8 = lax.broadcasted_iota(jnp.int32, (8, TOK), 0)
    before = jnp.where(
        lax.broadcasted_iota(jnp.int32, (TOK, TOK), 0) < lax.broadcasted_iota(jnp.int32, (TOK, TOK), 1),
        1.0, 0.0,
    ).astype(BF16)
    expert8 = ((2 * lax.rem(row8, 4) + c) * 16 + 2 * z + row8 // 4).astype(F32)
    rank8 = row8.astype(F32)
    zero8 = jnp.zeros((8, TOK), F32)

    def build(k, carry):
        zs = step_z(z, k)
        for s in range(2):
            hits, gates = [], []
            for cs in range(2):
                one = meta[zs, lax.rem(xp + s, 2) * 2 + cs]
                hit_sum, gate_sum = zero8, zero8
                for kk in range(8):
                    hit = one[kk : kk + 1, :] == expert8
                    hit_sum += jnp.where(hit, 1.0, 0.0)
                    gate_sum += jnp.where(hit, one[8 + kk : 9 + kk, :], 0.0)
                hits.append(hit_sum)
                gates.append(gate_sum)
            hit16 = jnp.concatenate(hits, axis=0)
            rank = jnp.dot(hit16.astype(BF16), before, preferred_element_type=F32)
            rank = jnp.where(hit16 > 0.5, rank, -1.0)
            picks, gate_picks = [], []
            for m in range(8):
                for cs in range(2):
                    at = rank[cs * 8 + m : cs * 8 + m + 1, :] == rank8
                    pick = jnp.where(at, 1.0, 0.0)
                    gate_pick = jnp.where(at, gates[cs][m : m + 1, :], 0.0)
                    pair_of = (lambda t: [t, zero8]) if cs == 0 else (lambda t: [zero8, t])
                    picks.append(jnp.concatenate(pair_of(pick), axis=1))
                    gate_picks.append(jnp.concatenate(pair_of(gate_pick), axis=1))
            sel[k, s] = jnp.concatenate(picks, axis=0).astype(BF16)
            weighted = jnp.concatenate(gate_picks, axis=0).astype(BF16)
            gate_row = nt(jnp.ones((16, 2 * TOK), BF16), weighted)
            gvb[s, pl.ds(zs, 1), :] = gate_row[0:1]
        return carry

    lax.fori_loop(0, NZ, build, 0)

    def gv_copy(m):
        return remote(
            gvb, gvr.at[me8], gv_s.at[m], gv_r.at[me8], dev(entry_x(m // 4), m % 4, z, c)
        )

    gvr[me8] = gvb[...]
    for m in range(8):
        @pl.when(m != me8)
        def _(m=m):
            gv_copy(m).start()

    def z_arrive(k):
        zs = step_z(z, k)

        @pl.when(k <= 6)
        def _():
            for part in range(2):
                landed(tx.at[zs, own_rows, part_cols[part]], zr_r.at[k, part])

        @pl.when(k == 7)
        def _():
            for part in range(2):
                landed(tx.at[zs, own_rows, pl.ds(part * HALF, HALF)], zr_r.at[k, part])

        odd = lax.rem(k, 2) == 1

        @pl.when((k <= 4) & odd)
        def _():
            for part in range(2):
                zsend(zs, part_cols[part], zr_s.at[k, part], zr_r.at[k + 2, part], 1).start()

        @pl.when((k <= 4) & jnp.logical_not(odd))
        def _():
            for part in range(2):
                zsend(zs, part_cols[part], zr_s.at[k, part], zr_r.at[k + 2, part], -1).start()

        @pl.when(k == 5)
        def _():
            zsend(zs, pl.ds(0, HALF), zr_s.at[5, 0], zr_r.at[7, 0], 1).start()

        @pl.when(k == 6)
        def _():
            zsend(zs, pl.ds(HALF, HALF), zr_s.at[6, 0], zr_r.at[7, 1], -1).start()

        for part in range(2):
            sib_copy(zs, k, part).start()

    def row_of(q, i, ys):
        return pl.multiple_of(((q * 2 + i) * 4 + ys) * 16, 16)

    def fh_pair(k, zs, m, part):
        b = lax.rem(k, NB)
        src_rows = pl.ds(m * 16, 16)
        if part == 0:
            src = stage.at[b, src_rows, pl.ds(0, D)]
            dst = rows.at[zs, pl.ds(row_of(qx, pair, y), 16), pl.ds(0, D)]
        else:
            src = stage.at[b, src_rows, pl.ds(D, CG)]
            dst = rows.at[zs, pl.ds(row_of(1 - qx, pair, y), 16), pl.ds(CA, CG)]
        return src, dst

    def fh_copy(k, zs, m, part):
        src, dst = fh_pair(k, zs, m, part)
        return remote(
            src, dst, fh_s.at[lax.rem(k, NB), m * 2 + part], fh_r.at[k, me8 * 2 + part],
            dev(entry_x(m // 4), m % 4, z, c),
        )

    def fh_start(k, zs):
        for m in range(8):
            for part in range(2):
                @pl.when(m != me8)
                def _(m=m, part=part):
                    fh_copy(k, zs, m, part).start()

                @pl.when(m == me8)
                def _(m=m, part=part):
                    src, dst = fh_pair(k, zs, m, part)
                    pltpu.make_async_copy(src, dst, fh_r.at[k, me8 * 2 + part]).start()

    def fh_sent(k):
        for m in range(8):
            for part in range(2):
                @pl.when(m != me8)
                def _(m=m, part=part):
                    fh_copy(k, step_z(z, k), m, part).wait_send()

    def fh_landed(k, zs):
        for j in range(8):
            landed(
                rows.at[zs, pl.ds(row_of(qx, j // 4, j % 4), 16), pl.ds(0, D)], fh_r.at[k, j * 2]
            )
            landed(
                rows.at[zs, pl.ds(row_of(1 - qx, j // 4, j % 4), 16), pl.ds(CA, CG)],
                fh_r.at[k, j * 2 + 1],
            )

    def fw_copy(k, zs):
        ref = rows.at[zs, pl.ds(pl.multiple_of(qx * 128, 128), 128), pl.ds(0, CA)]
        return remote(ref, ref, fw_s.at[k], fw_r.at[k], partner)

    def gather(k, zs):
        b = lax.rem(k, NB)

        def tile(t, carry):
            s = jnp.where(t >= D // CT, 1, 0)
            cols = pl.ds(pl.multiple_of(t * CT, CT), CT)
            picked = jnp.dot(sel[k, s], tx[zs, :, cols], preferred_element_type=F32)
            stage[b, :, cols] = picked.astype(BF16)
            return carry

        lax.fori_loop(0, TW // CT, tile, 0)

    def chunk(k, zs):
        lane = lax.broadcasted_iota(jnp.int32, (256, 128), 1)
        row = lax.broadcasted_iota(jnp.int32, (256, 128), 0)
        mine16 = lane == me8 * 16 + lax.rem(row, 16)
        gate_rows = []
        for q in range(2):
            for j in range(8):
                one = gvr[j, lax.rem(qx + q, 2), pl.ds(zs, 1), :]
                gate_rows.append(jnp.broadcast_to(one, (16, 128)))
        picked = jnp.where(mine16, jnp.concatenate(gate_rows, axis=0), 0.0).astype(BF16)
        gate_s[...] = jnp.dot(picked, jnp.ones((128, 128), BF16), preferred_element_type=F32)

        def ktile(t, carry):
            cols = pl.ds(pl.multiple_of(t * 512, 512), 512)
            part = nt(rows[zs, :, cols], wv[:, cols])

            @pl.when(t == 0)
            def _():
                proj[...] = part

            @pl.when(t > 0)
            def _():
                proj[...] += part

            return carry

        lax.fori_loop(0, D // 512, ktile, 0)

        total = jnp.zeros((256, 128), F32)
        for ct in range(4):
            cols = pl.ds(ct * 128, 128)
            gate = gate_s[...]
            pr = proj[:, cols]
            blocks = [
                actv[pl.ds(pl.multiple_of(ns * 256 + zs * 32, 32), 32), cols].astype(F32) for ns in range(8)
            ]
            pieces = []
            for q in range(2):
                for i in range(2):
                    xs = q + i * (3 - 2 * q)
                    for ns in range(8):
                        pieces.append(blocks[ns][xs * 8 : xs * 8 + 8])
            act = jnp.concatenate(pieces, axis=0)
            total += act * pr
            hidden = gate * pr
            for ns in range(8):
                back = []
                for xs in range(4):
                    at = ((((xs % 2) + (xs // 2)) % 2 * 2 + xs // 2) * 8 + ns) * 8
                    back.append(hidden[at : at + 8])
                hgv[pl.ds(pl.multiple_of(ns * 256 + zs * 32, 32), 32), cols] = jnp.concatenate(
                    back, axis=0
                ).astype(BF16)
            sct[ct * 128 : ct * 128 + 128, :] = jnp.transpose(gate * act).astype(BF16)
        ones = jnp.ones((16, 128), BF16)
        hi = total.astype(BF16)
        rest = total - hi.astype(F32)
        mid = rest.astype(BF16)
        low = (rest - mid.astype(F32)).astype(BF16)
        sums = nt(ones, hi) + nt(ones, mid) + nt(ones, low)
        for q in range(2):
            pv[q, pl.ds(zs, 1), :] = sums[0:1, q * 128 : q * 128 + 128]

        def ctile(t, carry):
            cols = pl.ds(pl.multiple_of(t * CT, CT), CT)
            part = jnp.dot(sct[...], rows[zs, :, cols], preferred_element_type=F32)

            @pl.when(k == 0)
            def _():
                wg[:, cols] = part

            @pl.when(k > 0)
            def _():
                wg[:, cols] += part

            return carry

        lax.fori_loop(0, D // CT, ctile, 0)

    def body(k, carry):
        @pl.when(k <= 7)
        def _():
            zs = step_z(z, k)

            @pl.when(lax.rem(k, 2) == 1)
            def _():
                z_arrive(k)

                @pl.when(k < 7)
                def _():
                    z_arrive(k + 1)

            for part in range(2):
                landed(tx.at[zs, sib_rows, part_cols[part]], sib_r.at[k, part])

            @pl.when(k >= NB)
            def _():
                fh_sent(k - NB)

            gather(k, zs)
            fh_start(k, zs)

        @pl.when((k >= 1) & (k <= 8))
        def _():
            zs = step_z(z, k - 1)
            fh_landed(k - 1, zs)
            fw_copy(k - 1, zs).start()

        @pl.when(k == 2)
        def _():
            act_copy.wait()
            w_copy.wait()
            for j in range(8):
                @pl.when(j != me8)
                def _(j=j):
                    landed(gvr.at[j], gv_r.at[j])

        @pl.when(k >= 2)
        def _():
            zs = step_z(z, k - 2)
            other = pl.ds(pl.multiple_of((1 - qx) * 128, 128), 128)
            landed(rows.at[zs, other, pl.ds(0, CA)], fw_r.at[k - 2])
            chunk(k - 2, zs)

        return carry

    lax.fori_loop(0, NZ + 2, body, 0)

    hg_copy = pltpu.make_async_copy(hgv, hg_hbm, in_sem.at[1])
    hg_copy.start()

    def square(t, acc):
        w = wg[:, pl.ds(pl.multiple_of(t * CT, CT), CT)]
        s = jnp.sum((w * w).reshape(FFH // 8, 8, CT), axis=0)
        return acc + s[:, :128] + s[:, 128:]

    squares = lax.fori_loop(0, D // CT, square, jnp.zeros((8, 128), F32))
    a1[0] = pv[1 - qx]
    a1[1] = squares
    e1 = remote(a1, b1, e1_s, e1_r, partner)
    e1.start()
    own = meta[z, mine]
    ranks = []
    for m in range(8):
        for cc in range(2):
            expert = ((2 * (m % 4) + cc) * 16 + m // 4 + 2 * row8).astype(F32)
            hit_sum = zero8
            for kk in range(8):
                hit_sum += jnp.where(own[kk : kk + 1, :] == expert, 1.0, 0.0)
            ranks.append(hit_sum)
    hit128 = jnp.concatenate(ranks, axis=0)
    rank = jnp.dot(hit128.astype(BF16), before, preferred_element_type=F32)
    rk_s[...] = jnp.where(hit128 > 0.5, rank, -1.0)
    e1.wait_recv()
    back = pv[qx] + b1[0]
    squares = a1[1] + b1[1]
    for j in range(8):
        a2[j, 0] = jnp.concatenate(
            [back[:, j * 16 : j * 16 + 16], jnp.zeros((8, 112), F32)], axis=1
        )
        a2[j, 1] = squares

    def e2_copy(j):
        return remote(a2.at[j], b2.at[me8], e2_s.at[j], e2_r.at[me8], dev(entry_x(j // 4), j % 4, z, c))

    for j in range(8):
        @pl.when(j != me8)
        def _(j=j):
            e2_copy(j).start()
    b2[me8] = a2[me8]
    for j in range(8):
        @pl.when(j != me8)
        def _(j=j):
            landed(b2.at[j], e2_r.at[j])
    a3[0] = jnp.concatenate([b2[j, 0][:, 0:16] for j in range(8)], axis=1)
    total = b2[0, 1]
    for j in range(1, 8):
        total += b2[j, 1]
    a3[1] = total
    e3 = [remote(a3, b3.at[z], e3_s.at[d], e3_r.at[d], zpeer(d)) for d in range(1, NZ)]
    for cp in e3:
        cp.start()
    b3[z] = a3[...]
    for d in range(1, NZ):
        landed(b3.at[lax.rem(z - d + NZ, NZ)], e3_r.at[d])
    a4[0] = jnp.concatenate([b3[j, 0, pl.ds(z, 1), :] for j in range(NZ)], axis=0)
    total = b3[0, 1]
    for j in range(1, NZ):
        total += b3[j, 1]
    a4[1] = total
    e4 = remote(a4, b4, e4_s, e4_r, sibling)
    e4.start()

    for part in range(2):
        zsend(z, part_cols[part], zr_s.at[0, part], zr_r.at[1, part], 1).wait_send()
        zsend(z, part_cols[part], zr_s.at[7, part], zr_r.at[2, part], -1).wait_send()
        for k in range(1, 5):
            zsend(step_z(z, k), part_cols[part], zr_s.at[k, part], zr_r.at[k + 2, part], 1).wait_send()
        for k in range(NZ):
            sib_copy(step_z(z, k), k, part).wait_send()
    zsend(step_z(z, 5), pl.ds(0, HALF), zr_s.at[5, 0], zr_r.at[7, 0], 1).wait_send()
    zsend(step_z(z, 6), pl.ds(HALF, HALF), zr_s.at[6, 0], zr_r.at[7, 1], -1).wait_send()
    pre.wait_send()

    e4.wait_recv()
    total = jnp.sum(a4[1] + b4[1], keepdims=True)
    factor = CLIP / jnp.sqrt(total / ENTRIES + EPS)
    out_copies = []
    for j in range(4):
        block = pl.ds((j % 2) * TOK, TOK)

        def scale(t, carry, j=j, block=block):
            cols = pl.ds(pl.multiple_of(t * 512, 512), 512)
            tx[j // 2, block, cols] = (wg[j * TOK : j * TOK + TOK, cols] * factor).astype(BF16)
            return carry

        lax.fori_loop(0, D // 512, scale, 0)
        cp = pltpu.make_async_copy(
            tx.at[j // 2, block, pl.ds(0, D)], out_hbm.at[pl.ds(j * TOK, TOK)], out_sem.at[j]
        )
        cp.start()
        out_copies.append(cp)

    first = jnp.where(c == 0, a4[0], b4[0])
    second = jnp.where(c == 0, b4[0], a4[0])
    values = []
    for v in (first, second):
        shifted = jnp.concatenate([v[:, 8:], v[:, :8]], axis=1)
        values.append(jnp.where(c == 0, v, shifted))
    sums = [zero8] * 8
    for m in range(8):
        for cc in range(2):
            at = (m * 2 + cc) * 8
            rk = rk_s[at : at + 8, :]
            val = zero8
            for r in range(8):
                col = jnp.broadcast_to(values[cc][:, m * 16 + r : m * 16 + r + 1], (8, TOK))
                val += jnp.where(rk == float(r), col, 0.0)
            expert = ((2 * (m % 4) + cc) * 16 + m // 4 + 2 * row8).astype(F32)
            for kk in range(8):
                sums[kk] += jnp.where(own[kk : kk + 1, :] == expert, val, 0.0)
    router_ref[...] = jnp.concatenate([jnp.sum(s, axis=0, keepdims=True) for s in sums], axis=0)

    for cp in meta_copies + zmeta + [e1] + e3 + [e4]:
        cp.wait_send()
    for k in range(NZ - NB, NZ):
        fh_sent(k)
    for k in range(NZ):
        fw_copy(k, step_z(z, k)).wait_send()
    for m in range(8):
        @pl.when(m != me8)
        def _(m=m):
            gv_copy(m).wait_send()
            e2_copy(m).wait_send()
    hg_copy.wait()
    for cp in out_copies:
        cp.wait()


def per_device(grad_out, expert_ids, gate_probs, down_weight, hidden_act):
    anywhere = pl.BlockSpec(memory_space=pl.ANY)
    vmem = pl.BlockSpec(memory_space=pltpu.VMEM)
    dma = pltpu.SemaphoreType.DMA
    small = pltpu.VMEM((2, 8, 128), F32)
    clipped, hidden_grad, router = pl.pallas_call(
        kernel,
        out_shape=(
            jax.ShapeDtypeStruct((FFH, D), BF16),
            jax.ShapeDtypeStruct((SLOTS, FFH), BF16),
            jax.ShapeDtypeStruct((8, TOK), F32),
        ),
        in_specs=[anywhere, vmem, vmem, anywhere, anywhere],
        out_specs=(anywhere, anywhere, vmem),
        scratch_shapes=[
            pltpu.VMEM((NZ, 2 * TOK, TW), BF16),
            pltpu.VMEM((NZ, 256, D), BF16),
            pltpu.VMEM((NB, 128, TW), BF16),
            pltpu.VMEM((FFH, D), BF16),
            pltpu.VMEM((SLOTS, FFH), BF16),
            pltpu.VMEM((SLOTS, FFH), BF16),
            pltpu.VMEM((FFH, D), F32),
            pltpu.VMEM((NZ, 2, 128, 256), BF16),
            pltpu.VMEM((NZ, 4, 16, 128), F32),
            small,
            pltpu.VMEM((8, 2, 8, 128), F32),
            pltpu.VMEM((256, FFH), F32),
            pltpu.VMEM((FFH, 256), BF16),
            pltpu.VMEM((256, 128), F32),
            pltpu.VMEM((128, 128), F32),
            small,
            small,
            small,
            pltpu.VMEM((8, 2, 8, 128), F32),
            pltpu.VMEM((8, 2, 8, 128), F32),
            small,
            pltpu.VMEM((8, 2, 8, 128), F32),
            small,
            small,
            dma((3,)),
            dma((4,)),
            dma((3,)),
            dma((3,)),
            dma((NZ,)),
            dma((NZ,)),
            dma,
            dma,
            dma((NZ, 2)),
            dma((NZ, 2)),
            dma((NZ, 2)),
            dma((NZ, 2)),
            dma((NB, 16)),
            dma((NZ, 16)),
            dma((NZ,)),
            dma((NZ,)),
            dma((8,)),
            dma((8,)),
            dma,
            dma,
            dma((8,)),
            dma((8,)),
            dma((NZ,)),
            dma((NZ,)),
            dma,
            dma,
        ],
        compiler_params=pltpu.CompilerParams(
            collective_id=0, has_side_effects=True, vmem_limit_bytes=60 * 2**20
        ),
    )(grad_out, expert_ids.T, gate_probs.T, down_weight, hidden_act)
    return clipped, hidden_grad, router.T


def solution(mesh):
    both = ("node", "local")
    return jax.shard_map(
        per_device,
        mesh=mesh,
        in_specs=(P(both, None), P(both, None), P(both, None), P(both, None), P(None, both)),
        out_specs=(P(both, None), P(None, both), P(both, None)),
        check_vma=False,
    )
```

```python
import jax
import jax.numpy as jnp
from jax import lax
from jax.experimental import pallas as pl
from jax.experimental.pallas import tpu as pltpu
from jax.sharding import PartitionSpec as P

MESH = pl.DeviceIdType.MESH
F32 = jnp.float32
BF16 = jnp.bfloat16

D = 3584
FFH = 512
TOK = 128
SLOTS = 2048
ENTRIES = 469762048
CLIP = 0.25
EPS = 1e-06

DH = D // 2
GH = 640
AH = DH - GH
TW = DH + GH
NB = 6
NZ = 8
STEPS = 2 * NZ


def nt(a, b):
    return lax.dot_general(a, b, (((1,), (1,)), ((), ())), preferred_element_type=F32)


def step_z(z, k):
    return lax.rem(z + ((k + 1) // 2) * (1 - 2 * lax.rem(k, 2)) + NZ, NZ)


def step_kh(j):
    g, u = (j + 2) // 4, lax.rem(j + 2, 4)
    mid = (g + 3) // 4 - g // 4
    h = mid * (u // 2) + (1 - mid) * lax.rem(u, 2)
    side = mid * lax.rem(u, 2)
    return mid * (2 * g - 1 + side) + (g // 4) * 7, h, side


def tiles(width):
    out, at = [], 0
    while at < width:
        size = min(256, width - at)
        out.append((at, size))
        at += size
    return out


def kernel(
    tok_hbm, ids_ref, gate_ref, w_hbm, act_hbm,
    wg_hbm, hg_hbm, router_ref, factor_ref,
    tx, rows, stage, wv, actv, hgv, wg, sel, meta, gvb, gvr, proj, sct, gate_s, rk_s,
    pv, a1, b1, a3, b3,
    in_sem, out_sem, meta_s, meta_r, zmeta_s, zmeta_r, pc_s, pc_r, zr_s, zr_r, sib_s, sib_r,
    fh_s, fh_r, fh_l, fw_s, fw_r, gv_s, gv_r, e1_s, e1_r, e3_s, e3_r,
):
    node = lax.axis_index("node")
    local = lax.axis_index("local")
    y, c = node // 2, lax.rem(node, 2)
    z, x = local // 4, lax.rem(local, 4)
    xp = lax.rem(x, 2)
    pair = x // 2
    qx = lax.rem(xp + pair, 2)
    x_partner = x + 1 - 2 * xp
    me8 = pair * 4 + y
    me16 = x * 4 + y

    def dev(xx, yy, zz, cc):
        return (2 * yy + cc, 4 * zz + xx)

    partner = dev(x_partner, y, z, c)
    sibling = dev(x, y, z, 1 - c)
    diagonal = dev(x_partner, y, z, 1 - c)

    def entry_x(p):
        return qx + p * (3 - 2 * qx)

    def remote(src, dst, ss, rs, to):
        return pltpu.make_async_remote_copy(
            src_ref=src, dst_ref=dst, send_sem=ss, recv_sem=rs, device_id=to, device_id_type=MESH
        )

    def landed(dst, rs):
        pltpu.make_async_copy(dst, dst, rs).wait()

    def zpeer(d, cc=None):
        return dev(x, y, lax.rem(z + d + NZ, NZ), c if cc is None else cc)

    own_rows = pl.ds(pl.multiple_of(c * TOK, TOK), TOK)
    sib_rows = pl.ds(pl.multiple_of((1 - c) * TOK, TOK), TOK)
    tok_copies = [
        pltpu.make_async_copy(
            tok_hbm.at[:, pl.ds(h * DH, DH)], tx.at[z, h, own_rows, pl.ds(0, DH)], in_sem.at[h]
        )
        for h in range(2)
    ]
    for cp in tok_copies:
        cp.start()
    act_copy = pltpu.make_async_copy(act_hbm, actv, in_sem.at[2])
    w_copy = pltpu.make_async_copy(w_hbm, wv, in_sem.at[3])
    act_copy.start()
    w_copy.start()
    mine = xp * 2 + c
    meta[z, mine] = jnp.concatenate(
        [ids_ref[...].astype(F32), gate_ref[...].astype(F32)], axis=0
    ).astype(BF16)

    barrier = pltpu.get_barrier_semaphore()

    def greet(to):
        pl.semaphore_signal(barrier, inc=1, device_id=to, device_id_type=MESH)

    for j in range(16):
        @pl.when(j != me16)
        def _(j=j):
            greet(dev(j // 4, j % 4, z, c))
    greet(sibling)
    greet(diagonal)
    for d in range(1, NZ):
        greet(zpeer(d))
        greet(zpeer(d, 1 - c))
    pl.semaphore_wait(barrier, 15 + 2 + 14)

    others = ((partner, (1 - xp) * 2 + c), (sibling, xp * 2 + 1 - c), (diagonal, (1 - xp) * 2 + 1 - c))
    meta_copies = [
        remote(meta.at[z, mine], meta.at[z, mine], meta_s.at[j], meta_r.at[j], to)
        for j, (to, _) in enumerate(others)
    ]
    for cp in meta_copies:
        cp.start()
    part_cols = (pl.ds(0, DH), pl.ds(DH, GH))
    pre = [
        remote(
            tx.at[z, h, own_rows, pl.ds(AH, GH)], tx.at[z, h, own_rows, pl.ds(DH, GH)],
            pc_s.at[h], pc_r.at[h], partner,
        )
        for h in range(2)
    ]

    def zsend(zs, h, part, ss, rs, d):
        ref = tx.at[zs, h, own_rows, part_cols[part]]
        return remote(ref, ref, ss, rs, zpeer(d))

    def sib_copy(zs, k, h, part):
        ref = tx.at[zs, h, own_rows, part_cols[part]]
        return remote(ref, ref, sib_s.at[k, h, part], sib_r.at[k, h, part], sibling)

    def own_sends(h, part):
        return (
            zsend(z, h, part, zr_s.at[0, h, part], zr_r.at[1, h, part], 1),
            zsend(z, h, part, zr_s.at[7, h, part], zr_r.at[2, h, part], -1),
            sib_copy(z, 0, h, part),
        )

    for h in range(2):
        tok_copies[h].wait()
        pre[h].start()
    for j, (_, slot) in enumerate(others):
        landed(meta.at[z, slot], meta_r.at[j])
    zmeta = [
        remote(meta.at[z], meta.at[z], zmeta_s.at[d], zmeta_r.at[d], zpeer(d)) for d in range(1, NZ)
    ]
    for cp in zmeta:
        cp.start()
    for cp in own_sends(0, 0):
        cp.start()

    row8 = lax.broadcasted_iota(jnp.int32, (8, TOK), 0)
    before = jnp.where(
        lax.broadcasted_iota(jnp.int32, (TOK, TOK), 0) < lax.broadcasted_iota(jnp.int32, (TOK, TOK), 1),
        1.0, 0.0,
    ).astype(BF16)
    expert8 = ((2 * lax.rem(row8, 4) + c) * 16 + 2 * z + row8 // 4).astype(F32)
    rank8 = row8.astype(F32)
    zero8 = jnp.zeros((8, TOK), F32)

    def build(k, carry):
        zs = step_z(z, k)
        for s in range(2):
            hits, gates = [], []
            for cs in range(2):
                one = meta[zs, lax.rem(xp + s, 2) * 2 + cs].astype(F32)
                hit_sum, gate_sum = zero8, zero8
                for kk in range(8):
                    hit = one[kk : kk + 1, :] == expert8
                    hit_sum += jnp.where(hit, 1.0, 0.0)
                    gate_sum += jnp.where(hit, one[8 + kk : 9 + kk, :], 0.0)
                hits.append(hit_sum)
                gates.append(gate_sum)
            hit16 = jnp.concatenate(hits, axis=0)
            rank = jnp.dot(hit16.astype(BF16), before, preferred_element_type=F32)
            rank = jnp.where(hit16 > 0.5, rank, -1.0)
            picks, gate_picks = [], []
            for m in range(8):
                for cs in range(2):
                    at = rank[cs * 8 + m : cs * 8 + m + 1, :] == rank8
                    pick = jnp.where(at, 1.0, 0.0)
                    gate_pick = jnp.where(at, gates[cs][m : m + 1, :], 0.0)
                    pair_of = (lambda t: [t, zero8]) if cs == 0 else (lambda t: [zero8, t])
                    picks.append(jnp.concatenate(pair_of(pick), axis=1))
                    gate_picks.append(jnp.concatenate(pair_of(gate_pick), axis=1))
            sel[k, s] = jnp.concatenate(picks, axis=0).astype(BF16)
            weighted = jnp.concatenate(gate_picks, axis=0).astype(BF16)
            gate_row = nt(jnp.ones((16, 2 * TOK), BF16), weighted)
            gvb[s, pl.ds(zs, 1), :] = gate_row[0:1]
        return carry

    def gv_copy(m):
        return remote(
            gvb, gvr.at[me8], gv_s.at[m], gv_r.at[me8], dev(entry_x(m // 4), m % 4, z, c)
        )

    build(0, 0)
    for h in range(2):
        if h:
            for cp in own_sends(h, 0):
                cp.start()
        pre[h].wait_recv()
        for cp in own_sends(h, 1):
            cp.start()
    wg[...] = jnp.zeros((FFH, D), F32)

    def z_arrive(k, h):
        zs = step_z(z, k)
        for part in range(2):
            landed(tx.at[zs, h, own_rows, part_cols[part]], zr_r.at[k, h, part])
        odd = lax.rem(k, 2)
        onward = (k <= 4) | ((k == 5) & (h == 0)) | ((k == 6) & (h == 1))
        to_k = k + 2 - k // 6

        @pl.when(onward & (odd == 1))
        def _():
            for part in range(2):
                zsend(zs, h, part, zr_s.at[k, h, part], zr_r.at[to_k, h, part], 1).start()

        @pl.when(onward & (odd == 0))
        def _():
            for part in range(2):
                zsend(zs, h, part, zr_s.at[k, h, part], zr_r.at[to_k, h, part], -1).start()

        for part in range(2):
            sib_copy(zs, k, h, part).start()

    def row_of(q, i, ys):
        return pl.multiple_of(((q * 2 + i) * 4 + ys) * 16, 16)

    def half(h, at, width):
        return pl.ds(pl.multiple_of(h * DH + at, 128), width)

    def fh_pair(j, m, part):
        k, h, _ = step_kh(j)
        zs = step_z(z, k)
        b = lax.rem(j, NB)
        src = stage.at[b, pl.ds(m * 16, 16), part_cols[part]]
        if part == 0:
            return src, rows.at[zs, pl.ds(row_of(qx, pair, y), 16), half(h, 0, DH)]
        return src, rows.at[zs, pl.ds(row_of(1 - qx, pair, y), 16), half(h, AH, GH)]

    def fh_start(j):
        b = lax.rem(j, NB)
        for part in range(2):
            for m in range(8):
                src, dst = fh_pair(j, m, part)

                @pl.when(m != me8)
                def _(m=m, src=src, dst=dst):
                    remote(src, dst, fh_s.at[b], fh_r.at[j], dev(entry_x(m // 4), m % 4, z, c)).start()

                @pl.when(m == me8)
                def _(src=src, dst=dst):
                    pltpu.make_async_copy(src, dst, fh_l.at[b]).start()

    def fh_sent(j):
        b = lax.rem(j, NB)
        landed(stage.at[b, pl.ds(0, 112)], fh_s.at[b])

    def fh_landed(j):
        b = lax.rem(j, NB)
        landed(stage.at[b, pl.ds(0, 112)], fh_r.at[j])
        landed(stage.at[b, pl.ds(0, 16)], fh_l.at[b])

    def fw_copy(j):
        k, h, _ = step_kh(j)
        ref = rows.at[step_z(z, k), pl.ds(pl.multiple_of(qx * 128, 128), 128), half(h, 0, AH)]
        return remote(ref, ref, fw_s.at[j], fw_r.at[j], partner)

    def gather(j):
        k, h, _ = step_kh(j)
        zs = step_z(z, k)
        b = lax.rem(j, NB)
        for s, (start, width) in enumerate(((0, DH), (DH, GH))):
            pick = sel[k, s]
            for at, size in tiles(width):
                cols = pl.ds(start + at, size)
                picked = jnp.dot(pick, tx[zs, h, :, cols], preferred_element_type=F32)
                stage[b, :, cols] = picked.astype(BF16)

    def acts(zs, cols):
        blocks = [
            actv[pl.ds(pl.multiple_of(ns * 256 + zs * 32, 32), 32), cols].astype(F32) for ns in range(8)
        ]
        pieces = []
        for q in range(2):
            for i in range(2):
                xs = q + i * (3 - 2 * q)
                for ns in range(8):
                    pieces.append(blocks[ns][xs * 8 : xs * 8 + 8])
        return jnp.concatenate(pieces, axis=0)

    def chunk(j):
        k, h, _ = step_kh(j)
        zs = step_z(z, k)
        slot = lax.rem(k, 2)

        @pl.when(h == 0)
        def _():
            lane = lax.broadcasted_iota(jnp.int32, (256, 128), 1)
            row = lax.broadcasted_iota(jnp.int32, (256, 128), 0)
            mine16 = lane == me8 * 16 + lax.rem(row, 16)
            gate_rows = []
            for q in range(2):
                for i in range(8):
                    one = gvr[i, lax.rem(qx + q, 2), pl.ds(zs, 1), :]
                    gate_rows.append(jnp.broadcast_to(one, (16, 128)))
            picked = jnp.where(mine16, jnp.concatenate(gate_rows, axis=0), 0.0).astype(BF16)
            gate = jnp.dot(picked, jnp.ones((128, 128), BF16), preferred_element_type=F32)
            gate_s[slot] = gate
            for ct in range(4):
                cols = pl.ds(ct * 128, 128)
                sct[slot, ct * 128 : ct * 128 + 128, :] = jnp.transpose(gate * acts(zs, cols)).astype(BF16)
            proj[slot] = jnp.zeros((256, FFH), F32)

        proj[slot] += nt(rows[zs, :, half(h, 0, DH)], wv[:, half(h, 0, DH)])

        @pl.when(h == 1)
        def _():
            total = jnp.zeros((256, 128), F32)
            for ct in range(4):
                cols = pl.ds(ct * 128, 128)
                pr = proj[slot, :, cols]
                total += acts(zs, cols) * pr
                hidden = gate_s[slot] * pr
                for ns in range(8):
                    back = []
                    for xs in range(4):
                        at = ((((xs % 2) + (xs // 2)) % 2 * 2 + xs // 2) * 8 + ns) * 8
                        back.append(hidden[at : at + 8])
                    hgv[pl.ds(pl.multiple_of(ns * 256 + zs * 32, 32), 32), cols] = jnp.concatenate(
                        back, axis=0
                    ).astype(BF16)
            ones = jnp.ones((16, 128), BF16)
            hi = total.astype(BF16)
            rest = total - hi.astype(F32)
            mid = rest.astype(BF16)
            low = (rest - mid.astype(F32)).astype(BF16)
            sums = nt(ones, hi) + nt(ones, mid) + nt(ones, low)
            for q in range(2):
                pv[q, pl.ds(zs, 1), :] = sums[0:1, q * 128 : q * 128 + 128]

        for at, size in tiles(DH):
            cols = half(h, at, size)
            wg[:, cols] += jnp.dot(sct[slot], rows[zs, :, cols], preferred_element_type=F32)

    def body(j, carry):
        @pl.when(j < STEPS)
        def _():
            k, h, side = step_kh(j)
            zs = step_z(z, k)

            @pl.when(j == 1)
            def _():
                for d in range(1, NZ):
                    landed(meta.at[lax.rem(z - d + NZ, NZ)], zmeta_r.at[d])
                lax.fori_loop(1, NZ, build, 0)
                gvr[me8] = gvb[...]
                for m in range(8):
                    @pl.when(m != me8)
                    def _(m=m):
                        gv_copy(m).start()

            @pl.when((k > 0) & (side == 0))
            def _():
                z_arrive(k, h)

                @pl.when(k < 7)
                def _():
                    z_arrive(k + 1, h)

            for part in range(2):
                landed(tx.at[zs, h, sib_rows, part_cols[part]], sib_r.at[k, h, part])

            @pl.when(j >= NB)
            def _():
                fh_sent(j - NB)

            gather(j)
            fh_start(j)

        @pl.when((j >= 1) & (j <= STEPS))
        def _():
            fh_landed(j - 1)
            fw_copy(j - 1).start()

        @pl.when(j == 2)
        def _():
            act_copy.wait()
            w_copy.wait()
            for i in range(8):
                @pl.when(i != me8)
                def _(i=i):
                    landed(gvr.at[i], gv_r.at[i])

        @pl.when(j >= 2)
        def _():
            k, h, _ = step_kh(j - 2)
            other = pl.ds(pl.multiple_of((1 - qx) * 128, 128), 128)
            landed(rows.at[step_z(z, k), other, half(h, 0, AH)], fw_r.at[j - 2])
            chunk(j - 2)

        return carry

    lax.fori_loop(0, STEPS + 2, body, 0)

    out_copies = [
        pltpu.make_async_copy(wg, wg_hbm, out_sem.at[0]),
        pltpu.make_async_copy(hgv, hg_hbm, out_sem.at[1]),
    ]
    for cp in out_copies:
        cp.start()

    squares = zero8
    for at, size in tiles(D):
        w = wg[:, at : at + size]
        s = jnp.sum((w * w).reshape(FFH // 8, 8, size), axis=0)
        squares += s[:, :128] + s[:, 128:]
    for j in range(16):
        xx, yy = j // 4, j % 4
        back = pv[(xx % 2 + xx // 2) % 2]
        lanes = (xx // 2 * 4 + yy) * 16
        a1[j, 0] = jnp.concatenate([back[:, lanes : lanes + 16], jnp.zeros((8, 112), F32)], axis=1)
        a1[j, 1] = squares

    def e1_copy(j):
        return remote(a1.at[j], b1.at[me16], e1_s.at[j], e1_r.at[me16], dev(j // 4, j % 4, z, c))

    for j in range(16):
        @pl.when(j != me16)
        def _(j=j):
            e1_copy(j).start()
    b1[me16] = a1[me16]

    own = meta[z, mine].astype(F32)
    ranks = []
    for m in range(8):
        for cc in range(2):
            expert = ((2 * (m % 4) + cc) * 16 + m // 4 + 2 * row8).astype(F32)
            hit_sum = zero8
            for kk in range(8):
                hit_sum += jnp.where(own[kk : kk + 1, :] == expert, 1.0, 0.0)
            ranks.append(hit_sum)
    hit128 = jnp.concatenate(ranks, axis=0)
    rank = jnp.dot(hit128.astype(BF16), before, preferred_element_type=F32)
    rk_s[...] = jnp.where(hit128 > 0.5, rank, -1.0)

    for j in range(16):
        @pl.when(j != me16)
        def _(j=j):
            landed(b1.at[j], e1_r.at[j])
    a3[0] = jnp.concatenate(
        [
            b1[2 * p * 4 + yy, 0][:, 0:16] + b1[(2 * p + 1) * 4 + yy, 0][:, 0:16]
            for p in range(2)
            for yy in range(4)
        ],
        axis=1,
    )
    total = b1[0, 1]
    for j in range(1, 16):
        total += b1[j, 1]
    a3[1] = total

    def e3_copy(d, cc):
        to_c = c if cc == 0 else 1 - c
        return remote(
            a3, b3.at[z, c], e3_s.at[d, cc], e3_r.at[d, cc], zpeer(d, to_c)
        )

    e3 = [e3_copy(d, cc) for d in range(NZ) for cc in range(2) if d or cc]
    for cp in e3:
        cp.start()
    b3[z, c] = a3[...]
    for d in range(NZ):
        for cc in range(2):
            if d or cc:
                from_c = c if cc == 0 else 1 - c
                landed(b3.at[lax.rem(z - d + NZ, NZ), from_c], e3_r.at[d, cc])
    total = zero8
    for zz in range(NZ):
        for cc in range(2):
            total += b3[zz, cc, 1]
    total = jnp.sum(total, keepdims=True)
    factor_ref[...] = jnp.broadcast_to(CLIP / jnp.sqrt(total / ENTRIES + EPS), (8, 128))

    values = []
    for cc in range(2):
        v = jnp.concatenate([b3[zz, cc, 0, pl.ds(z, 1), :] for zz in range(NZ)], axis=0)
        shifted = jnp.concatenate([v[:, 8:], v[:, :8]], axis=1)
        values.append(jnp.where(c == 0, v, shifted))
    sums = [zero8] * 8
    for m in range(8):
        for cc in range(2):
            at = (m * 2 + cc) * 8
            rk = rk_s[at : at + 8, :]
            val = zero8
            for r in range(8):
                col = jnp.broadcast_to(values[cc][:, m * 16 + r : m * 16 + r + 1], (8, TOK))
                val += jnp.where(rk == float(r), col, 0.0)
            expert = ((2 * (m % 4) + cc) * 16 + m // 4 + 2 * row8).astype(F32)
            for kk in range(8):
                sums[kk] += jnp.where(own[kk : kk + 1, :] == expert, val, 0.0)
    router_ref[...] = jnp.concatenate([jnp.sum(s, axis=0, keepdims=True) for s in sums], axis=0)

    for cp in meta_copies + zmeta + pre + e3:
        cp.wait_send()
    for h in range(2):
        for part in range(2):
            for cp in own_sends(h, part):
                cp.wait_send()
            for k in range(1, NZ):
                sib_copy(step_z(z, k), k, h, part).wait_send()
                if k <= 4 or (k == 5 and h == 0) or (k == 6 and h == 1):
                    zsend(
                        step_z(z, k), h, part, zr_s.at[k, h, part], zr_r.at[7, h, part], 1
                    ).wait_send()
    for j in range(STEPS - NB, STEPS):
        fh_sent(j)
    for j in range(STEPS):
        fw_copy(j).wait_send()
    for m in range(8):
        @pl.when(m != me8)
        def _(m=m):
            gv_copy(m).wait_send()
    for j in range(16):
        @pl.when(j != me16)
        def _(j=j):
            e1_copy(j).wait_send()
    for cp in out_copies:
        cp.wait()


BLOCKS = 8
BR = FFH // BLOCKS


def finish(wg_hbm, hg_hbm, router_in, factor_ref, out_hbm, hg_out, router_out, wide, narrow, sems, out_sems, hg_sem):
    hg_copy = pltpu.make_async_copy(hg_hbm, hg_out, hg_sem)
    loads = [
        pltpu.make_async_copy(wg_hbm.at[pl.ds(j * BR, BR)], wide.at[j], sems.at[j]) for j in range(BLOCKS)
    ]
    stores = [
        pltpu.make_async_copy(narrow.at[j], out_hbm.at[pl.ds(j * BR, BR)], out_sems.at[j]) for j in range(BLOCKS)
    ]
    for cp in loads:
        cp.start()
    hg_copy.start()
    router_out[...] = router_in[...]
    factor = factor_ref[0:1, 0:1]
    for j in range(BLOCKS):
        loads[j].wait()
        narrow[j] = (wide[j] * factor).astype(BF16)
        stores[j].start()
    for cp in stores:
        cp.wait()
    hg_copy.wait()


def per_device(grad_out, expert_ids, gate_probs, down_weight, hidden_act):
    anywhere = pl.BlockSpec(memory_space=pl.ANY)
    vmem = pl.BlockSpec(memory_space=pltpu.VMEM)
    dma = pltpu.SemaphoreType.DMA
    small = pltpu.VMEM((2, 8, 128), F32)
    weight_grad, hidden, router, factor = pl.pallas_call(
        kernel,
        out_shape=(
            jax.ShapeDtypeStruct((FFH, D), F32),
            jax.ShapeDtypeStruct((SLOTS, FFH), BF16),
            jax.ShapeDtypeStruct((8, TOK), F32),
            jax.ShapeDtypeStruct((8, 128), F32),
        ),
        in_specs=[anywhere, vmem, vmem, anywhere, anywhere],
        out_specs=(anywhere, anywhere, vmem, vmem),
        scratch_shapes=[
            pltpu.VMEM((NZ, 2, 2 * TOK, TW), BF16),
            pltpu.VMEM((NZ, 256, D), BF16),
            pltpu.VMEM((NB, 128, TW), BF16),
            pltpu.VMEM((FFH, D), BF16),
            pltpu.VMEM((SLOTS, FFH), BF16),
            pltpu.VMEM((SLOTS, FFH), BF16),
            pltpu.VMEM((FFH, D), F32),
            pltpu.VMEM((NZ, 2, 128, 256), BF16),
            pltpu.VMEM((NZ, 4, 16, 128), BF16),
            small,
            pltpu.VMEM((8, 2, 8, 128), F32),
            pltpu.VMEM((2, 256, FFH), F32),
            pltpu.VMEM((2, FFH, 256), BF16),
            pltpu.VMEM((2, 256, 128), F32),
            pltpu.VMEM((128, 128), F32),
            small,
            pltpu.VMEM((16, 2, 8, 128), F32),
            pltpu.VMEM((16, 2, 8, 128), F32),
            small,
            pltpu.VMEM((NZ, 2, 2, 8, 128), F32),
            dma((4,)),
            dma((2,)),
            dma((3,)),
            dma((3,)),
            dma((NZ,)),
            dma((NZ,)),
            dma((2,)),
            dma((2,)),
            dma((NZ, 2, 2)),
            dma((NZ, 2, 2)),
            dma((NZ, 2, 2)),
            dma((NZ, 2, 2)),
            dma((NB,)),
            dma((STEPS,)),
            dma((NB,)),
            dma((STEPS,)),
            dma((STEPS,)),
            dma((8,)),
            dma((8,)),
            dma((16,)),
            dma((16,)),
            dma((NZ, 2)),
            dma((NZ, 2)),
        ],
        compiler_params=pltpu.CompilerParams(
            collective_id=0, has_side_effects=True, vmem_limit_bytes=60 * 2**20
        ),
    )(grad_out, expert_ids.T, gate_probs.T, down_weight, hidden_act)
    clipped, hidden_grad, router = pl.pallas_call(
        finish,
        out_shape=(
            jax.ShapeDtypeStruct((FFH, D), BF16),
            jax.ShapeDtypeStruct((SLOTS, FFH), BF16),
            jax.ShapeDtypeStruct((8, TOK), F32),
        ),
        in_specs=[anywhere, anywhere, vmem, vmem],
        out_specs=(anywhere, anywhere, vmem),
        scratch_shapes=[
            pltpu.VMEM((BLOCKS, BR, D), F32),
            pltpu.VMEM((BLOCKS, BR, D), BF16),
            dma((BLOCKS,)),
            dma((BLOCKS,)),
            dma,
        ],
        compiler_params=pltpu.CompilerParams(vmem_limit_bytes=32 * 2**20),
    )(weight_grad, hidden, router, factor)
    return clipped, hidden_grad, router.T


def solution(mesh):
    both = ("node", "local")
    return jax.shard_map(
        per_device,
        mesh=mesh,
        in_specs=(P(both, None), P(both, None), P(both, None), P(both, None), P(None, both)),
        out_specs=(P(both, None), P(None, both), P(both, None)),
        check_vma=False,
    )
```

```python
import jax
import jax.numpy as jnp
from jax import lax
from jax.experimental import pallas as pl
from jax.experimental.pallas import tpu as pltpu
from jax.sharding import PartitionSpec as P

MESH = pl.DeviceIdType.MESH
F32 = jnp.float32
BF16 = jnp.bfloat16

D = 3584
FFH = 512
TOK = 128
SLOTS = 2048
ENTRIES = 469762048
CLIP = 0.25
EPS = 1e-06

DH = D // 2
GH = 640
AH = DH - GH
TW = DH + GH
NB = 6
NZ = 8
STEPS = 2 * NZ
LF = 2
LC = 4


def nt(a, b):
    return lax.dot_general(a, b, (((1,), (1,)), ((), ())), preferred_element_type=F32)


def step_z(z, k):
    return lax.rem(z + ((k + 1) // 2) * (1 - 2 * lax.rem(k, 2)) + NZ, NZ)


def step_kh(j):
    g, u = (j + 2) // 4, lax.rem(j + 2, 4)
    mid = (g + 3) // 4 - g // 4
    h = mid * (u // 2) + (1 - mid) * lax.rem(u, 2)
    side = mid * lax.rem(u, 2)
    return mid * (2 * g - 1 + side) + (g // 4) * 7, h, side


def tiles(width):
    out, at = [], 0
    while at < width:
        size = min(256, width - at)
        out.append((at, size))
        at += size
    return out


def kernel(
    tok_hbm, ids_ref, gate_ref, w_hbm, act_hbm,
    wg_hbm, hg_hbm, router_ref, factor_ref,
    tx, rows, stage, wv, actv, hgv, wg, sel, meta, metaz, gvb, gvr, proj, sct, gate_s, rk_s,
    pv, a1, b1, a3, b3,
    in_sem, out_sem, meta_s, meta_r, zmeta_s, zmeta_r, pack_s, pack_r, pc_s, pc_r, zr_s, zr_r, sib_s, sib_r,
    fh_s, fh_r, fh_l, fw_s, fw_r, gv_s, gv_r, e1_s, e1_r, e3_s, e3_r,
):
    node = lax.axis_index("node")
    local = lax.axis_index("local")
    y, c = node // 2, lax.rem(node, 2)
    z, x = local // 4, lax.rem(local, 4)
    xp = lax.rem(x, 2)
    pair = x // 2
    qx = lax.rem(xp + pair, 2)
    x_partner = x + 1 - 2 * xp
    me8 = pair * 4 + y
    me16 = x * 4 + y

    def dev(xx, yy, zz, cc):
        return (2 * yy + cc, 4 * zz + xx)

    partner = dev(x_partner, y, z, c)
    sibling = dev(x, y, z, 1 - c)
    diagonal = dev(x_partner, y, z, 1 - c)

    def entry_x(p):
        return qx + p * (3 - 2 * qx)

    def remote(src, dst, ss, rs, to):
        return pltpu.make_async_remote_copy(
            src_ref=src, dst_ref=dst, send_sem=ss, recv_sem=rs, device_id=to, device_id_type=MESH
        )

    def landed(dst, rs):
        pltpu.make_async_copy(dst, dst, rs).wait()

    def zpeer(d, cc=None):
        return dev(x, y, lax.rem(z + d + NZ, NZ), c if cc is None else cc)

    own_rows = pl.ds(pl.multiple_of(c * TOK, TOK), TOK)
    sib_rows = pl.ds(pl.multiple_of((1 - c) * TOK, TOK), TOK)
    tok_copies = [
        pltpu.make_async_copy(
            tok_hbm.at[:, pl.ds(h * DH, DH)], tx.at[z, h, own_rows, pl.ds(0, DH)], in_sem.at[h]
        )
        for h in range(2)
    ]
    for cp in tok_copies:
        cp.start()
    act_copy = pltpu.make_async_copy(act_hbm, actv, in_sem.at[2])
    w_copy = pltpu.make_async_copy(w_hbm, wv, in_sem.at[3])
    act_copy.start()
    w_copy.start()
    mine = xp * 2 + c
    routing = jnp.concatenate([ids_ref[...].astype(F32), gate_ref[...].astype(F32)], axis=0).astype(BF16)
    meta[mine] = routing
    metaz[mine, z] = routing

    barrier = pltpu.get_barrier_semaphore()

    def greet(to):
        pl.semaphore_signal(barrier, inc=1, device_id=to, device_id_type=MESH)

    for j in range(16):
        @pl.when(j != me16)
        def _(j=j):
            greet(dev(j // 4, j % 4, z, c))
    greet(sibling)
    greet(diagonal)
    for d in range(1, NZ):
        greet(zpeer(d))
        greet(zpeer(d, 1 - c))
    pl.semaphore_wait(barrier, 15 + 2 + 14)

    others = ((partner, (1 - xp) * 2 + c), (sibling, xp * 2 + 1 - c), (diagonal, (1 - xp) * 2 + 1 - c))
    meta_copies = [
        remote(meta.at[mine], meta.at[mine], meta_s.at[j], meta_r.at[j], to)
        for j, (to, _) in enumerate(others)
    ]
    zmeta = [
        remote(metaz.at[mine, z], metaz.at[mine, z], zmeta_s.at[d], zmeta_r.at[d], zpeer(d))
        for d in range(1, NZ)
    ]
    packs = [
        remote(metaz.at[mine], metaz.at[mine], pack_s.at[j], pack_r.at[j], to)
        for j, (to, _) in enumerate(others)
    ]
    for cp in meta_copies + zmeta:
        cp.start()
    part_cols = (pl.ds(0, DH), pl.ds(DH, GH))
    pre = [
        remote(
            tx.at[z, h, own_rows, pl.ds(AH, GH)], tx.at[z, h, own_rows, pl.ds(DH, GH)],
            pc_s.at[h], pc_r.at[h], partner,
        )
        for h in range(2)
    ]

    def zsend(zs, h, part, ss, rs, d):
        ref = tx.at[zs, h, own_rows, part_cols[part]]
        return remote(ref, ref, ss, rs, zpeer(d))

    def sib_copy(zs, k, h, part):
        ref = tx.at[zs, h, own_rows, part_cols[part]]
        return remote(ref, ref, sib_s.at[k, h, part], sib_r.at[k, h, part], sibling)

    def own_zsends(h, part):
        return (
            zsend(z, h, part, zr_s.at[0, h, part], zr_r.at[1, h, part], 1),
            zsend(z, h, part, zr_s.at[7, h, part], zr_r.at[2, h, part], -1),
        )

    for h in range(2):
        tok_copies[h].wait()
        pre[h].start()
        sib_copy(z, 0, h, 0).start()
        if h == 0:
            for cp in own_zsends(0, 0):
                cp.start()

    row8 = lax.broadcasted_iota(jnp.int32, (8, TOK), 0)
    before = jnp.where(
        lax.broadcasted_iota(jnp.int32, (TOK, TOK), 0) < lax.broadcasted_iota(jnp.int32, (TOK, TOK), 1),
        1.0, 0.0,
    ).astype(BF16)
    expert8 = ((2 * lax.rem(row8, 4) + c) * 16 + 2 * z + row8 // 4).astype(F32)
    rank8 = row8.astype(F32)
    zero8 = jnp.zeros((8, TOK), F32)

    def build_from(data, k):
        zs = step_z(z, k)
        for s in range(2):
            hits, gates = [], []
            for cs in range(2):
                one = data(lax.rem(xp + s, 2) * 2 + cs, zs).astype(F32)
                hit_sum, gate_sum = zero8, zero8
                for kk in range(8):
                    hit = one[kk : kk + 1, :] == expert8
                    hit_sum += jnp.where(hit, 1.0, 0.0)
                    gate_sum += jnp.where(hit, one[8 + kk : 9 + kk, :], 0.0)
                hits.append(hit_sum)
                gates.append(gate_sum)
            hit16 = jnp.concatenate(hits, axis=0)
            rank = jnp.dot(hit16.astype(BF16), before, preferred_element_type=F32)
            rank = jnp.where(hit16 > 0.5, rank, -1.0)
            picks, gate_picks = [], []
            for m in range(8):
                for cs in range(2):
                    at = rank[cs * 8 + m : cs * 8 + m + 1, :] == rank8
                    pick = jnp.where(at, 1.0, 0.0)
                    gate_pick = jnp.where(at, gates[cs][m : m + 1, :], 0.0)
                    pair_of = (lambda t: [t, zero8]) if cs == 0 else (lambda t: [zero8, t])
                    picks.append(jnp.concatenate(pair_of(pick), axis=1))
                    gate_picks.append(jnp.concatenate(pair_of(gate_pick), axis=1))
            sel[k, s] = jnp.concatenate(picks, axis=0).astype(BF16)
            weighted = jnp.concatenate(gate_picks, axis=0).astype(BF16)
            gate_row = nt(jnp.ones((16, 2 * TOK), BF16), weighted)
            gvb[s, pl.ds(zs, 1), :] = gate_row[0:1]

    def build(k, carry):
        build_from(lambda who, zs: metaz[who, zs], k)
        return carry

    def gv_copy(m):
        return remote(
            gvb, gvr.at[me8], gv_s.at[m], gv_r.at[me8], dev(entry_x(m // 4), m % 4, z, c)
        )

    def z_arrive(k, h):
        zs = step_z(z, k)
        for part in range(2):
            landed(tx.at[zs, h, own_rows, part_cols[part]], zr_r.at[k, h, part])
        odd = lax.rem(k, 2)
        onward = (k <= 4) | ((k == 5) & (h == 0)) | ((k == 6) & (h == 1))
        to_k = k + 2 - k // 6

        @pl.when(onward & (odd == 1))
        def _():
            for part in range(2):
                zsend(zs, h, part, zr_s.at[k, h, part], zr_r.at[to_k, h, part], 1).start()

        @pl.when(onward & (odd == 0))
        def _():
            for part in range(2):
                zsend(zs, h, part, zr_s.at[k, h, part], zr_r.at[to_k, h, part], -1).start()

        for part in range(2):
            sib_copy(zs, k, h, part).start()

    def row_of(q, i, ys):
        return pl.multiple_of(((q * 2 + i) * 4 + ys) * 16, 16)

    def half(h, at, width):
        return pl.ds(pl.multiple_of(h * DH + at, 128), width)

    def fh_pair(j, m, part):
        k, h, _ = step_kh(j)
        zs = step_z(z, k)
        b = lax.rem(j, NB)
        src = stage.at[b, pl.ds(pl.multiple_of(m * 16, 16), 16), part_cols[part]]
        if part == 0:
            return src, rows.at[zs, pl.ds(row_of(qx, pair, y), 16), half(h, 0, DH)]
        return src, rows.at[zs, pl.ds(row_of(1 - qx, pair, y), 16), half(h, AH, GH)]

    def fh_start(j, parts=(0, 1)):
        b = lax.rem(j, NB)
        for part in parts:
            for far, dy in ((1, 2), (0, 2), (1, 1), (1, 3), (0, 1), (0, 3), (1, 0), (0, 0)):
                yy = lax.rem(y + dy, 4)
                m = (pair + far - 2 * far * pair) * 4 + yy
                src, dst = fh_pair(j, m, part)
                if far or dy:
                    xx = x + far * (3 - 2 * x)
                    remote(src, dst, fh_s.at[b], fh_r.at[j], dev(xx, yy, z, c)).start()
                else:
                    pltpu.make_async_copy(src, dst, fh_l.at[b]).start()

    def fh_sent(j):
        b = lax.rem(j, NB)
        landed(stage.at[b, pl.ds(0, 112)], fh_s.at[b])

    def fh_landed(j):
        b = lax.rem(j, NB)
        landed(stage.at[b, pl.ds(0, 112)], fh_r.at[j])
        landed(stage.at[b, pl.ds(0, 16)], fh_l.at[b])

    def fw_copy(j):
        k, h, _ = step_kh(j)
        ref = rows.at[step_z(z, k), pl.ds(pl.multiple_of(qx * 128, 128), 128), half(h, 0, AH)]
        return remote(ref, ref, fw_s.at[j], fw_r.at[j], partner)

    def gather(j, parts=(0, 1)):
        k, h, _ = step_kh(j)
        zs = step_z(z, k)
        b = lax.rem(j, NB)
        for s in parts:
            start, width = ((0, DH), (DH, GH))[s]
            pick = sel[k, s]
            for at, size in tiles(width):
                cols = pl.ds(start + at, size)
                picked = jnp.dot(pick, tx[zs, h, :, cols], preferred_element_type=F32)
                stage[b, :, cols] = picked.astype(BF16)

    def acts(zs, cols):
        blocks = [
            actv[pl.ds(pl.multiple_of(ns * 256 + zs * 32, 32), 32), cols].astype(F32) for ns in range(8)
        ]
        pieces = []
        for q in range(2):
            for i in range(2):
                xs = q + i * (3 - 2 * q)
                for ns in range(8):
                    pieces.append(blocks[ns][xs * 8 : xs * 8 + 8])
        return jnp.concatenate(pieces, axis=0)

    def chunk(j):
        k, h, _ = step_kh(j)
        zs = step_z(z, k)
        slot = lax.rem(k, 2)

        @pl.when(h == 0)
        def _():
            lane = lax.broadcasted_iota(jnp.int32, (256, 128), 1)
            row = lax.broadcasted_iota(jnp.int32, (256, 128), 0)
            mine16 = lane == me8 * 16 + lax.rem(row, 16)
            gate_rows = []
            for q in range(2):
                for i in range(8):
                    one = gvr[i, lax.rem(qx + q, 2), pl.ds(zs, 1), :]
                    gate_rows.append(jnp.broadcast_to(one, (16, 128)))
            picked = jnp.where(mine16, jnp.concatenate(gate_rows, axis=0), 0.0).astype(BF16)
            gate = jnp.dot(picked, jnp.ones((128, 128), BF16), preferred_element_type=F32)
            gate_s[slot] = gate
            for ct in range(4):
                cols = pl.ds(ct * 128, 128)
                sct[slot, ct * 128 : ct * 128 + 128, :] = jnp.transpose(gate * acts(zs, cols)).astype(BF16)
            proj[slot] = jnp.zeros((256, FFH), F32)

        proj[slot] += nt(rows[zs, :, half(h, 0, DH)], wv[:, half(h, 0, DH)])

        @pl.when(h == 1)
        def _():
            total = jnp.zeros((256, 128), F32)
            for ct in range(4):
                cols = pl.ds(ct * 128, 128)
                pr = proj[slot, :, cols]
                total += acts(zs, cols) * pr
                hidden = gate_s[slot] * pr
                for ns in range(8):
                    back = []
                    for xs in range(4):
                        at = ((((xs % 2) + (xs // 2)) % 2 * 2 + xs // 2) * 8 + ns) * 8
                        back.append(hidden[at : at + 8])
                    hgv[pl.ds(pl.multiple_of(ns * 256 + zs * 32, 32), 32), cols] = jnp.concatenate(
                        back, axis=0
                    ).astype(BF16)
            ones = jnp.ones((16, 128), BF16)
            hi = total.astype(BF16)
            rest = total - hi.astype(F32)
            mid = rest.astype(BF16)
            low = (rest - mid.astype(F32)).astype(BF16)
            sums = nt(ones, hi) + nt(ones, mid) + nt(ones, low)
            for q in range(2):
                pv[q, pl.ds(zs, 1), :] = sums[0:1, q * 128 : q * 128 + 128]

        for at, size in tiles(DH):
            cols = half(h, at, size)
            wg[:, cols] += jnp.dot(sct[slot], rows[zs, :, cols], preferred_element_type=F32)

    def body(j, carry):
        @pl.when(j < STEPS)
        def _():
            k, h, side = step_kh(j)
            zs = step_z(z, k)

            @pl.when((k > 0) & (side == 0))
            def _():
                z_arrive(k, h)

                @pl.when(k < 7)
                def _():
                    z_arrive(k + 1, h)

            for part in range(2):
                landed(tx.at[zs, h, sib_rows, part_cols[part]], sib_r.at[k, h, part])

            @pl.when(j >= NB)
            def _():
                fh_sent(j - NB)

            gather(j)
            fh_start(j)

        @pl.when(j == 1)
        def _():
            for d in range(1, NZ):
                landed(metaz.at[mine, lax.rem(z - d + NZ, NZ)], zmeta_r.at[d])
            for cp in packs:
                cp.start()

        @pl.when((j >= LF) & (j < STEPS + LF))
        def _():
            fh_landed(j - LF)
            fw_copy(j - LF).start()

        @pl.when(j == 1)
        def _():
            for i, (_, slot) in enumerate(others):
                landed(metaz.at[slot], pack_r.at[i])
            lax.fori_loop(1, NZ, build, 0)
            gvr[me8] = gvb[...]
            for m in range(8):
                @pl.when(m != me8)
                def _(m=m):
                    gv_copy(m).start()
            wg[...] = jnp.zeros((FFH, D), F32)

        @pl.when(j == LC)
        def _():
            act_copy.wait()
            w_copy.wait()
            for i in range(8):
                @pl.when(i != me8)
                def _(i=i):
                    landed(gvr.at[i], gv_r.at[i])

        @pl.when(j >= LC)
        def _():
            k, h, _ = step_kh(j - LC)
            other = pl.ds(pl.multiple_of((1 - qx) * 128, 128), 128)
            landed(rows.at[step_z(z, k), other, half(h, 0, AH)], fw_r.at[j - LC])
            chunk(j - LC)

        return carry

    for j, (_, slot) in enumerate(others):
        landed(meta.at[slot], meta_r.at[j])
    build_from(lambda who, zs: meta[who], 0)
    for part in range(2):
        if part == 1:
            pre[0].wait_recv()
            for cp in own_zsends(0, 1):
                cp.start()
            sib_copy(z, 0, 0, 1).start()
            for cp in own_zsends(1, 0):
                cp.start()
        landed(tx.at[z, 0, sib_rows, part_cols[part]], sib_r.at[0, 0, part])
        gather(0, (part,))
        fh_start(0, (part,))
    pre[1].wait_recv()
    for cp in own_zsends(1, 1):
        cp.start()
    sib_copy(z, 0, 1, 1).start()
    lax.fori_loop(1, STEPS + LC, body, 0)

    out_copies = [
        pltpu.make_async_copy(wg, wg_hbm, out_sem.at[0]),
        pltpu.make_async_copy(hgv, hg_hbm, out_sem.at[1]),
    ]
    for cp in out_copies:
        cp.start()

    squares = zero8
    for at, size in tiles(D):
        w = wg[:, at : at + size]
        s = jnp.sum((w * w).reshape(FFH // 8, 8, size), axis=0)
        squares += s[:, :128] + s[:, 128:]
    for j in range(16):
        xx, yy = j // 4, j % 4
        back = pv[(xx % 2 + xx // 2) % 2]
        lanes = (xx // 2 * 4 + yy) * 16
        a1[j, 0] = jnp.concatenate([back[:, lanes : lanes + 16], jnp.zeros((8, 112), F32)], axis=1)
        a1[j, 1] = squares

    def e1_copy(j):
        return remote(a1.at[j], b1.at[me16], e1_s.at[j], e1_r.at[me16], dev(j // 4, j % 4, z, c))

    for j in range(16):
        @pl.when(j != me16)
        def _(j=j):
            e1_copy(j).start()
    b1[me16] = a1[me16]

    own = meta[mine].astype(F32)
    ranks = []
    for m in range(8):
        for cc in range(2):
            expert = ((2 * (m % 4) + cc) * 16 + m // 4 + 2 * row8).astype(F32)
            hit_sum = zero8
            for kk in range(8):
                hit_sum += jnp.where(own[kk : kk + 1, :] == expert, 1.0, 0.0)
            ranks.append(hit_sum)
    hit128 = jnp.concatenate(ranks, axis=0)
    rank = jnp.dot(hit128.astype(BF16), before, preferred_element_type=F32)
    rk_s[...] = jnp.where(hit128 > 0.5, rank, -1.0)

    for j in range(16):
        @pl.when(j != me16)
        def _(j=j):
            landed(b1.at[j], e1_r.at[j])
    a3[0] = jnp.concatenate(
        [
            b1[2 * p * 4 + yy, 0][:, 0:16] + b1[(2 * p + 1) * 4 + yy, 0][:, 0:16]
            for p in range(2)
            for yy in range(4)
        ],
        axis=1,
    )
    total = b1[0, 1]
    for j in range(1, 16):
        total += b1[j, 1]
    a3[1] = total

    def e3_copy(d, cc):
        to_c = c if cc == 0 else 1 - c
        return remote(
            a3, b3.at[z, c], e3_s.at[d, cc], e3_r.at[d, cc], zpeer(d, to_c)
        )

    e3 = [e3_copy(d, cc) for d in range(NZ) for cc in range(2) if d or cc]
    for cp in e3:
        cp.start()
    b3[z, c] = a3[...]
    for d in range(NZ):
        for cc in range(2):
            if d or cc:
                from_c = c if cc == 0 else 1 - c
                landed(b3.at[lax.rem(z - d + NZ, NZ), from_c], e3_r.at[d, cc])
    total = zero8
    for zz in range(NZ):
        for cc in range(2):
            total += b3[zz, cc, 1]
    total = jnp.sum(total, keepdims=True)
    factor_ref[...] = jnp.broadcast_to(CLIP / jnp.sqrt(total / ENTRIES + EPS), (8, 128))

    values = []
    for cc in range(2):
        v = jnp.concatenate([b3[zz, cc, 0, pl.ds(z, 1), :] for zz in range(NZ)], axis=0)
        shifted = jnp.concatenate([v[:, 8:], v[:, :8]], axis=1)
        values.append(jnp.where(c == 0, v, shifted))
    sums = [zero8] * 8
    for m in range(8):
        for cc in range(2):
            at = (m * 2 + cc) * 8
            rk = rk_s[at : at + 8, :]
            val = zero8
            for r in range(8):
                col = jnp.broadcast_to(values[cc][:, m * 16 + r : m * 16 + r + 1], (8, TOK))
                val += jnp.where(rk == float(r), col, 0.0)
            expert = ((2 * (m % 4) + cc) * 16 + m // 4 + 2 * row8).astype(F32)
            for kk in range(8):
                sums[kk] += jnp.where(own[kk : kk + 1, :] == expert, val, 0.0)
    router_ref[...] = jnp.concatenate([jnp.sum(s, axis=0, keepdims=True) for s in sums], axis=0)

    for cp in meta_copies + zmeta + packs + pre + e3:
        cp.wait_send()
    for h in range(2):
        for part in range(2):
            for cp in own_zsends(h, part):
                cp.wait_send()
            for k in range(NZ):
                sib_copy(step_z(z, k), k, h, part).wait_send()
                if 1 <= k <= 4 or (k == 5 and h == 0) or (k == 6 and h == 1):
                    zsend(
                        step_z(z, k), h, part, zr_s.at[k, h, part], zr_r.at[7, h, part], 1
                    ).wait_send()
    for j in range(STEPS - NB, STEPS):
        fh_sent(j)
    for j in range(STEPS):
        fw_copy(j).wait_send()
    for m in range(8):
        @pl.when(m != me8)
        def _(m=m):
            gv_copy(m).wait_send()
    for j in range(16):
        @pl.when(j != me16)
        def _(j=j):
            e1_copy(j).wait_send()
    for cp in out_copies:
        cp.wait()


BLOCKS = 8
BR = FFH // BLOCKS


def finish(wg_hbm, hg_hbm, router_in, factor_ref, out_hbm, hg_out, router_out, wide, narrow, hidden, sems, out_sems, hg_sem):
    hg_in = pltpu.make_async_copy(hg_hbm, hidden, hg_sem.at[0])
    hg_copy = pltpu.make_async_copy(hidden, hg_out, hg_sem.at[1])
    loads = [
        pltpu.make_async_copy(wg_hbm.at[pl.ds(j * BR, BR)], wide.at[j], sems.at[j]) for j in range(BLOCKS)
    ]
    stores = [
        pltpu.make_async_copy(narrow.at[j], out_hbm.at[pl.ds(j * BR, BR)], out_sems.at[j]) for j in range(BLOCKS)
    ]
    loads[0].start()
    hg_in.start()
    for cp in loads[1:]:
        cp.start()
    router_out[...] = router_in[...]
    factor = factor_ref[0:1, 0:1]
    for j in range(BLOCKS):
        loads[j].wait()
        narrow[j] = (wide[j] * factor).astype(BF16)
        stores[j].start()
        if j == 0:
            hg_in.wait()
            hg_copy.start()
    for cp in stores:
        cp.wait()
    hg_copy.wait()


def per_device(grad_out, expert_ids, gate_probs, down_weight, hidden_act):
    anywhere = pl.BlockSpec(memory_space=pl.ANY)
    vmem = pl.BlockSpec(memory_space=pltpu.VMEM)
    dma = pltpu.SemaphoreType.DMA
    small = pltpu.VMEM((2, 8, 128), F32)
    weight_grad, hidden, router, factor = pl.pallas_call(
        kernel,
        out_shape=(
            jax.ShapeDtypeStruct((FFH, D), F32),
            jax.ShapeDtypeStruct((SLOTS, FFH), BF16),
            jax.ShapeDtypeStruct((8, TOK), F32),
            jax.ShapeDtypeStruct((8, 128), F32),
        ),
        in_specs=[anywhere, vmem, vmem, anywhere, anywhere],
        out_specs=(anywhere, anywhere, vmem, vmem),
        scratch_shapes=[
            pltpu.VMEM((NZ, 2, 2 * TOK, TW), BF16),
            pltpu.VMEM((NZ, 256, D), BF16),
            pltpu.VMEM((NB, 128, TW), BF16),
            pltpu.VMEM((FFH, D), BF16),
            pltpu.VMEM((SLOTS, FFH), BF16),
            pltpu.VMEM((SLOTS, FFH), BF16),
            pltpu.VMEM((FFH, D), F32),
            pltpu.VMEM((NZ, 2, 128, 256), BF16),
            pltpu.VMEM((4, 16, 128), BF16),
            pltpu.VMEM((4, NZ, 16, 128), BF16),
            small,
            pltpu.VMEM((8, 2, 8, 128), F32),
            pltpu.VMEM((2, 256, FFH), F32),
            pltpu.VMEM((2, FFH, 256), BF16),
            pltpu.VMEM((2, 256, 128), F32),
            pltpu.VMEM((128, 128), F32),
            small,
            pltpu.VMEM((16, 2, 8, 128), F32),
            pltpu.VMEM((16, 2, 8, 128), F32),
            small,
            pltpu.VMEM((NZ, 2, 2, 8, 128), F32),
            dma((4,)),
            dma((2,)),
            dma((3,)),
            dma((3,)),
            dma((NZ,)),
            dma((NZ,)),
            dma((3,)),
            dma((3,)),
            dma((2,)),
            dma((2,)),
            dma((NZ, 2, 2)),
            dma((NZ, 2, 2)),
            dma((NZ, 2, 2)),
            dma((NZ, 2, 2)),
            dma((NB,)),
            dma((STEPS,)),
            dma((NB,)),
            dma((STEPS,)),
            dma((STEPS,)),
            dma((8,)),
            dma((8,)),
            dma((16,)),
            dma((16,)),
            dma((NZ, 2)),
            dma((NZ, 2)),
        ],
        compiler_params=pltpu.CompilerParams(
            collective_id=0, has_side_effects=True, vmem_limit_bytes=60 * 2**20
        ),
    )(grad_out, expert_ids.T, gate_probs.T, down_weight, hidden_act)
    clipped, hidden_grad, router = pl.pallas_call(
        finish,
        out_shape=(
            jax.ShapeDtypeStruct((FFH, D), BF16),
            jax.ShapeDtypeStruct((SLOTS, FFH), BF16),
            jax.ShapeDtypeStruct((8, TOK), F32),
        ),
        in_specs=[anywhere, anywhere, vmem, vmem],
        out_specs=(anywhere, anywhere, vmem),
        scratch_shapes=[
            pltpu.VMEM((BLOCKS, BR, D), F32),
            pltpu.VMEM((BLOCKS, BR, D), BF16),
            pltpu.VMEM((SLOTS, FFH), BF16),
            dma((BLOCKS,)),
            dma((BLOCKS,)),
            dma((2,)),
        ],
        compiler_params=pltpu.CompilerParams(vmem_limit_bytes=60 * 2**20),
    )(weight_grad, hidden, router, factor)
    return clipped, hidden_grad, router.T


def solution(mesh):
    both = ("node", "local")
    return jax.shard_map(
        per_device,
        mesh=mesh,
        in_specs=(P(both, None), P(both, None), P(both, None), P(both, None), P(None, both)),
        out_specs=(P(both, None), P(None, both), P(both, None)),
        check_vma=False,
    )
```

```python
import jax
import jax.numpy as jnp
from jax import lax
from jax.experimental import pallas as pl
from jax.experimental.pallas import tpu as pltpu
from jax.sharding import PartitionSpec as P

MESH = pl.DeviceIdType.MESH
F32 = jnp.float32
BF16 = jnp.bfloat16

D = 3584
FFH = 512
TOK = 128
SLOTS = 2048
ENTRIES = 469762048
CLIP = 0.25
EPS = 1e-06

DH = D // 2
GH = 640
AH = DH - GH
TW = DH + GH
NB = 6
NZ = 8
STEPS = 2 * NZ
PIECES = ((0, AH), (AH, GH), (DH, GH))
WAITS = ((0, AH), (AH, TW - AH))
LF = 2
LC = 4


def nt(a, b):
    return lax.dot_general(a, b, (((1,), (1,)), ((), ())), preferred_element_type=F32)


def step_z(z, k):
    return lax.rem(z + ((k + 1) // 2) * (1 - 2 * lax.rem(k, 2)) + NZ, NZ)


def step_kh(j):
    g, u = (j + 2) // 4, lax.rem(j + 2, 4)
    mid = (g + 3) // 4 - g // 4
    h = mid * (u // 2) + (1 - mid) * lax.rem(u, 2)
    side = mid * lax.rem(u, 2)
    return mid * (2 * g - 1 + side) + (g // 4) * 7, h, side


def tiles(width):
    out, at = [], 0
    while at < width:
        size = min(256, width - at)
        out.append((at, size))
        at += size
    return out


def kernel(
    tok_hbm, ids_ref, gate_ref, w_hbm, act_hbm,
    wg_hbm, hg_hbm, router_ref, factor_ref,
    tx, rows, stage, wv, actv, hgv, wg, sel, meta, metaz, gvb, gvr, proj, sct, gate_s, rk_s, sq_s,
    pv, a1, b1, a3, b3,
    in_sem, out_sem, meta_s, meta_r, zmeta_s, zmeta_r, pack_s, pack_r, pc_s, pc_r, zr_s, zr_r, sib_s, sib_r,
    fh_s, fh_r, fh_l, fw_s, fw_r, gv_s, gv_r, e1_s, e1_r, e3_s, e3_r,
):
    node = lax.axis_index("node")
    local = lax.axis_index("local")
    y, c = node // 2, lax.rem(node, 2)
    z, x = local // 4, lax.rem(local, 4)
    xp = lax.rem(x, 2)
    pair = x // 2
    qx = lax.rem(xp + pair, 2)
    x_partner = x + 1 - 2 * xp
    me8 = pair * 4 + y
    me16 = x * 4 + y

    def dev(xx, yy, zz, cc):
        return (2 * yy + cc, 4 * zz + xx)

    partner = dev(x_partner, y, z, c)
    sibling = dev(x, y, z, 1 - c)
    diagonal = dev(x_partner, y, z, 1 - c)

    def entry_x(p):
        return qx + p * (3 - 2 * qx)

    def remote(src, dst, ss, rs, to):
        return pltpu.make_async_remote_copy(
            src_ref=src, dst_ref=dst, send_sem=ss, recv_sem=rs, device_id=to, device_id_type=MESH
        )

    def landed(dst, rs):
        pltpu.make_async_copy(dst, dst, rs).wait()

    def zpeer(d, cc=None):
        return dev(x, y, lax.rem(z + d + NZ, NZ), c if cc is None else cc)

    own_rows = pl.ds(pl.multiple_of(c * TOK, TOK), TOK)
    sib_rows = pl.ds(pl.multiple_of((1 - c) * TOK, TOK), TOK)
    tok_copies = [
        pltpu.make_async_copy(
            tok_hbm.at[:, pl.ds(h * DH, DH)], tx.at[z, h, own_rows, pl.ds(0, DH)], in_sem.at[h]
        )
        for h in range(2)
    ]
    for cp in tok_copies:
        cp.start()
    act_copy = pltpu.make_async_copy(act_hbm, actv, in_sem.at[2])
    w_copy = pltpu.make_async_copy(w_hbm, wv, in_sem.at[3])
    act_copy.start()
    w_copy.start()
    mine = xp * 2 + c
    routing = jnp.concatenate([ids_ref[...].astype(F32), gate_ref[...].astype(F32)], axis=0).astype(BF16)
    meta[mine] = routing
    metaz[mine, z] = routing

    barrier = pltpu.get_barrier_semaphore()

    def greet(to):
        pl.semaphore_signal(barrier, inc=1, device_id=to, device_id_type=MESH)

    for j in range(16):
        @pl.when(j != me16)
        def _(j=j):
            greet(dev(j // 4, j % 4, z, c))
    greet(sibling)
    greet(diagonal)
    for d in range(1, NZ):
        greet(zpeer(d))
        greet(zpeer(d, 1 - c))
    pl.semaphore_wait(barrier, 15 + 2 + 14)

    others = ((partner, (1 - xp) * 2 + c), (sibling, xp * 2 + 1 - c), (diagonal, (1 - xp) * 2 + 1 - c))
    meta_copies = [
        remote(meta.at[mine], meta.at[mine], meta_s.at[j], meta_r.at[j], to)
        for j, (to, _) in enumerate(others)
    ]
    zmeta = [
        remote(metaz.at[mine, z], metaz.at[mine, z], zmeta_s.at[d], zmeta_r.at[d], zpeer(d))
        for d in range(1, NZ)
    ]
    packs = [
        remote(metaz.at[mine], metaz.at[mine], pack_s.at[j], pack_r.at[j], to)
        for j, (to, _) in enumerate(others)
    ]
    for cp in meta_copies + zmeta:
        cp.start()
    part_cols = (pl.ds(0, DH), pl.ds(DH, GH))
    pre = [
        remote(
            tx.at[z, h, own_rows, pl.ds(AH, GH)], tx.at[z, h, own_rows, pl.ds(DH, GH)],
            pc_s.at[h], pc_r.at[h], partner,
        )
        for h in range(2)
    ]

    def zsend(zs, h, part, ss, rs, d):
        ref = tx.at[zs, h, own_rows, part_cols[part]]
        return remote(ref, ref, ss, rs, zpeer(d))

    def sib_copy(zs, k, h, part):
        ref = tx.at[zs, h, own_rows, part_cols[part]]
        return remote(ref, ref, sib_s.at[k, h, part], sib_r.at[k, h, part], sibling)

    def own_zsends(h, part):
        return (
            zsend(z, h, part, zr_s.at[0, h, part], zr_r.at[1, h, part], 1),
            zsend(z, h, part, zr_s.at[7, h, part], zr_r.at[2, h, part], -1),
        )

    for h in range(2):
        tok_copies[h].wait()
        pre[h].start()
        sib_copy(z, 0, h, 0).start()
        if h == 0:
            for cp in own_zsends(0, 0):
                cp.start()

    row8 = lax.broadcasted_iota(jnp.int32, (8, TOK), 0)
    before = jnp.where(
        lax.broadcasted_iota(jnp.int32, (TOK, TOK), 0) < lax.broadcasted_iota(jnp.int32, (TOK, TOK), 1),
        1.0, 0.0,
    ).astype(BF16)
    expert8 = ((2 * lax.rem(row8, 4) + c) * 16 + 2 * z + row8 // 4).astype(F32)
    rank8 = row8.astype(F32)
    zero8 = jnp.zeros((8, TOK), F32)

    def build_from(data, k):
        zs = step_z(z, k)
        for s in range(2):
            hits, gates = [], []
            for cs in range(2):
                one = data(lax.rem(xp + s, 2) * 2 + cs, zs).astype(F32)
                hit_sum, gate_sum = zero8, zero8
                for kk in range(8):
                    hit = one[kk : kk + 1, :] == expert8
                    hit_sum += jnp.where(hit, 1.0, 0.0)
                    gate_sum += jnp.where(hit, one[8 + kk : 9 + kk, :], 0.0)
                hits.append(hit_sum)
                gates.append(gate_sum)
            hit16 = jnp.concatenate(hits, axis=0)
            rank = jnp.dot(hit16.astype(BF16), before, preferred_element_type=F32)
            rank = jnp.where(hit16 > 0.5, rank, -1.0)
            picks, gate_picks = [], []
            for m in range(8):
                for cs in range(2):
                    at = rank[cs * 8 + m : cs * 8 + m + 1, :] == rank8
                    pick = jnp.where(at, 1.0, 0.0)
                    gate_pick = jnp.where(at, gates[cs][m : m + 1, :], 0.0)
                    pair_of = (lambda t: [t, zero8]) if cs == 0 else (lambda t: [zero8, t])
                    picks.append(jnp.concatenate(pair_of(pick), axis=1))
                    gate_picks.append(jnp.concatenate(pair_of(gate_pick), axis=1))
            sel[k, s] = jnp.concatenate(picks, axis=0).astype(BF16)
            weighted = jnp.concatenate(gate_picks, axis=0).astype(BF16)
            gate_row = nt(jnp.ones((16, 2 * TOK), BF16), weighted)
            gvb[s, pl.ds(zs, 1), :] = gate_row[0:1]

    def build(k, carry):
        build_from(lambda who, zs: metaz[who, zs], k)
        return carry

    def gv_copy(m):
        return remote(
            gvb, gvr.at[me8], gv_s.at[m], gv_r.at[me8], dev(entry_x(m // 4), m % 4, z, c)
        )

    def z_arrive(k, h):
        zs = step_z(z, k)
        for part in range(2):
            landed(tx.at[zs, h, own_rows, part_cols[part]], zr_r.at[k, h, part])
        odd = lax.rem(k, 2)
        onward = (k <= 4) | ((k == 5) & (h == 0)) | ((k == 6) & (h == 1))
        to_k = k + 2 - k // 6

        @pl.when(onward & (odd == 1))
        def _():
            for part in range(2):
                zsend(zs, h, part, zr_s.at[k, h, part], zr_r.at[to_k, h, part], 1).start()

        @pl.when(onward & (odd == 0))
        def _():
            for part in range(2):
                zsend(zs, h, part, zr_s.at[k, h, part], zr_r.at[to_k, h, part], -1).start()

        for part in range(2):
            sib_copy(zs, k, h, part).start()

    def row_of(q, i, ys):
        return pl.multiple_of(((q * 2 + i) * 4 + ys) * 16, 16)

    def half(h, at, width):
        return pl.ds(pl.multiple_of(h * DH + at, 128), width)

    def fh_pair(j, m, part):
        k, h, _ = step_kh(j)
        zs = step_z(z, k)
        b = lax.rem(j, NB)
        start, width = PIECES[part]
        src = stage.at[b, pl.ds(pl.multiple_of(m * 16, 16), 16), pl.ds(start, width)]
        source = 1 - qx if part == 2 else qx
        return src, rows.at[zs, pl.ds(row_of(source, pair, y), 16), half(h, min(start, AH), width)]

    def fh_start(j, parts):
        b = lax.rem(j, NB)
        for part in parts:
            for far, dy in ((1, 2), (0, 2), (1, 1), (1, 3), (0, 1), (0, 3), (1, 0), (0, 0)):
                yy = lax.rem(y + dy, 4)
                m = (pair + far - 2 * far * pair) * 4 + yy
                src, dst = fh_pair(j, m, part)
                if far or dy:
                    xx = x + far * (3 - 2 * x)
                    remote(src, dst, fh_s.at[b], fh_r.at[j, min(part, 1)], dev(xx, yy, z, c)).start()
                else:
                    pltpu.make_async_copy(src, dst, fh_l.at[b, min(part, 1)]).start()

    def fh_sent(j):
        b = lax.rem(j, NB)
        landed(stage.at[b, pl.ds(0, 112)], fh_s.at[b])

    def fh_landed(j, group):
        b = lax.rem(j, NB)
        cols = pl.ds(*WAITS[group])
        landed(stage.at[b, pl.ds(0, 112), cols], fh_r.at[j, group])
        landed(stage.at[b, pl.ds(0, 16), cols], fh_l.at[b, group])

    def fw_copy(j):
        k, h, _ = step_kh(j)
        ref = rows.at[step_z(z, k), pl.ds(pl.multiple_of(qx * 128, 128), 128), half(h, 0, AH)]
        return remote(ref, ref, fw_s.at[j], fw_r.at[j], partner)

    def gather(j, parts):
        k, h, _ = step_kh(j)
        zs = step_z(z, k)
        b = lax.rem(j, NB)
        for s in parts:
            start, width = ((0, DH), (DH, GH))[s]
            pick = sel[k, s]
            for at, size in tiles(width):
                cols = pl.ds(start + at, size)
                picked = jnp.dot(pick, tx[zs, h, :, cols], preferred_element_type=F32)
                stage[b, :, cols] = picked.astype(BF16)

    def acts(zs, cols):
        blocks = [
            actv[pl.ds(pl.multiple_of(ns * 256 + zs * 32, 32), 32), cols].astype(F32) for ns in range(8)
        ]
        pieces = []
        for q in range(2):
            for i in range(2):
                xs = q + i * (3 - 2 * q)
                for ns in range(8):
                    pieces.append(blocks[ns][xs * 8 : xs * 8 + 8])
        return jnp.concatenate(pieces, axis=0)

    def chunk(j):
        k, h, _ = step_kh(j)
        zs = step_z(z, k)
        slot = lax.rem(k, 2)

        @pl.when(h == 0)
        def _():
            lane = lax.broadcasted_iota(jnp.int32, (256, 128), 1)
            row = lax.broadcasted_iota(jnp.int32, (256, 128), 0)
            mine16 = lane == me8 * 16 + lax.rem(row, 16)
            gate_rows = []
            for q in range(2):
                for i in range(8):
                    one = gvr[i, lax.rem(qx + q, 2), pl.ds(zs, 1), :]
                    gate_rows.append(jnp.broadcast_to(one, (16, 128)))
            picked = jnp.where(mine16, jnp.concatenate(gate_rows, axis=0), 0.0).astype(BF16)
            gate = jnp.dot(picked, jnp.ones((128, 128), BF16), preferred_element_type=F32)
            gate_s[slot] = gate
            for ct in range(4):
                cols = pl.ds(ct * 128, 128)
                sct[slot, ct * 128 : ct * 128 + 128, :] = jnp.transpose(gate * acts(zs, cols)).astype(BF16)
            proj[slot] = jnp.zeros((256, FFH), F32)

        proj[slot] += nt(rows[zs, :, half(h, 0, DH)], wv[:, half(h, 0, DH)])

        @pl.when(h == 1)
        def _():
            total = jnp.zeros((256, 128), F32)
            for ct in range(4):
                cols = pl.ds(ct * 128, 128)
                pr = proj[slot, :, cols]
                total += acts(zs, cols) * pr
                hidden = gate_s[slot] * pr
                for ns in range(8):
                    back = []
                    for xs in range(4):
                        at = ((((xs % 2) + (xs // 2)) % 2 * 2 + xs // 2) * 8 + ns) * 8
                        back.append(hidden[at : at + 8])
                    hgv[pl.ds(pl.multiple_of(ns * 256 + zs * 32, 32), 32), cols] = jnp.concatenate(
                        back, axis=0
                    ).astype(BF16)
            ones = jnp.ones((16, 128), BF16)
            hi = total.astype(BF16)
            rest = total - hi.astype(F32)
            mid = rest.astype(BF16)
            low = (rest - mid.astype(F32)).astype(BF16)
            sums = nt(ones, hi) + nt(ones, mid) + nt(ones, low)
            for q in range(2):
                pv[q, pl.ds(zs, 1), :] = sums[0:1, q * 128 : q * 128 + 128]

        for at, size in tiles(DH):
            cols = half(h, at, size)
            wg[:, cols] += jnp.dot(sct[slot], rows[zs, :, cols], preferred_element_type=F32)

    def square(at):
        acc = zero8
        for start, size in tiles(DH):
            w = wg[:, at + start : at + start + size]
            s = jnp.sum((w * w).reshape(FFH // 8, 8, size), axis=0)
            acc += s[:, :128] + s[:, 128:]
        return acc

    def wg_copy(h):
        cols = pl.ds(h * DH, DH)
        return pltpu.make_async_copy(wg.at[:, cols], wg_hbm.at[:, cols], out_sem.at[h])

    def body(j, carry):
        @pl.when(j < STEPS)
        def _():
            k, h, side = step_kh(j)
            zs = step_z(z, k)

            @pl.when((k > 0) & (side == 0))
            def _():
                z_arrive(k, h)

                @pl.when(k < 7)
                def _():
                    z_arrive(k + 1, h)

            for part in range(2):
                landed(tx.at[zs, h, sib_rows, part_cols[part]], sib_r.at[k, h, part])

            @pl.when(j >= NB)
            def _():
                fh_sent(j - NB)

            gather(j, (0,))
            fh_start(j, (0, 1))
            gather(j, (1,))
            fh_start(j, (2,))

        @pl.when(j == 1)
        def _():
            for d in range(1, NZ):
                landed(metaz.at[mine, lax.rem(z - d + NZ, NZ)], zmeta_r.at[d])
            for cp in packs:
                cp.start()

        @pl.when((j >= LF) & (j < STEPS + LF))
        def _():
            fh_landed(j - LF, 0)
            fw_copy(j - LF).start()

        @pl.when(j == 1)
        def _():
            for i, (_, slot) in enumerate(others):
                landed(metaz.at[slot], pack_r.at[i])
            lax.fori_loop(1, NZ, build, 0)
            gvr[me8] = gvb[...]
            for m in range(8):
                @pl.when(m != me8)
                def _(m=m):
                    gv_copy(m).start()
            wg[...] = jnp.zeros((FFH, D), F32)

        @pl.when(j == LC)
        def _():
            act_copy.wait()
            w_copy.wait()
            for i in range(8):
                @pl.when(i != me8)
                def _(i=i):
                    landed(gvr.at[i], gv_r.at[i])

        @pl.when(j >= LC)
        def _():
            k, h, _ = step_kh(j - LC)
            other = pl.ds(pl.multiple_of((1 - qx) * 128, 128), 128)
            landed(rows.at[step_z(z, k), other, half(h, 0, AH)], fw_r.at[j - LC])
            fh_landed(j - LC, 1)
            chunk(j - LC)

        @pl.when(j == STEPS + LC - 2)
        def _():
            sq_s[...] = square(0)
            wg_copy(0).start()

        return carry

    for j, (_, slot) in enumerate(others):
        landed(meta.at[slot], meta_r.at[j])
    build_from(lambda who, zs: meta[who], 0)
    for part in range(2):
        if part == 1:
            pre[0].wait_recv()
            for cp in own_zsends(0, 1):
                cp.start()
            sib_copy(z, 0, 0, 1).start()
            for cp in own_zsends(1, 0):
                cp.start()
        landed(tx.at[z, 0, sib_rows, part_cols[part]], sib_r.at[0, 0, part])
        gather(0, (part,))
        fh_start(0, (0, 1) if part == 0 else (2,))
    pre[1].wait_recv()
    for cp in own_zsends(1, 1):
        cp.start()
    sib_copy(z, 0, 1, 1).start()
    lax.fori_loop(1, STEPS + LC, body, 0)

    hg_copy = pltpu.make_async_copy(hgv, hg_hbm, out_sem.at[2])
    wg_copy(1).start()
    hg_copy.start()

    squares = sq_s[...] + square(DH)
    for j in range(16):
        xx, yy = j // 4, j % 4
        back = pv[(xx % 2 + xx // 2) % 2]
        lanes = (xx // 2 * 4 + yy) * 16
        a1[j, 0] = jnp.concatenate([back[:, lanes : lanes + 16], jnp.zeros((8, 112), F32)], axis=1)
        a1[j, 1] = squares

    def e1_copy(j):
        return remote(a1.at[j], b1.at[me16], e1_s.at[j], e1_r.at[me16], dev(j // 4, j % 4, z, c))

    for j in range(16):
        @pl.when(j != me16)
        def _(j=j):
            e1_copy(j).start()
    b1[me16] = a1[me16]

    own = meta[mine].astype(F32)
    ranks = []
    for m in range(8):
        for cc in range(2):
            expert = ((2 * (m % 4) + cc) * 16 + m // 4 + 2 * row8).astype(F32)
            hit_sum = zero8
            for kk in range(8):
                hit_sum += jnp.where(own[kk : kk + 1, :] == expert, 1.0, 0.0)
            ranks.append(hit_sum)
    hit128 = jnp.concatenate(ranks, axis=0)
    rank = jnp.dot(hit128.astype(BF16), before, preferred_element_type=F32)
    rk_s[...] = jnp.where(hit128 > 0.5, rank, -1.0)

    for j in range(16):
        @pl.when(j != me16)
        def _(j=j):
            landed(b1.at[j], e1_r.at[j])
    a3[0] = jnp.concatenate(
        [
            b1[2 * p * 4 + yy, 0][:, 0:16] + b1[(2 * p + 1) * 4 + yy, 0][:, 0:16]
            for p in range(2)
            for yy in range(4)
        ],
        axis=1,
    )
    total = b1[0, 1]
    for j in range(1, 16):
        total += b1[j, 1]
    a3[1] = total

    def e3_copy(d, cc):
        to_c = c if cc == 0 else 1 - c
        return remote(
            a3, b3.at[z, c], e3_s.at[d, cc], e3_r.at[d, cc], zpeer(d, to_c)
        )

    e3 = [e3_copy(d, cc) for d in range(NZ) for cc in range(2) if d or cc]
    for cp in e3:
        cp.start()
    b3[z, c] = a3[...]
    for d in range(NZ):
        for cc in range(2):
            if d or cc:
                from_c = c if cc == 0 else 1 - c
                landed(b3.at[lax.rem(z - d + NZ, NZ), from_c], e3_r.at[d, cc])
    total = zero8
    for zz in range(NZ):
        for cc in range(2):
            total += b3[zz, cc, 1]
    total = jnp.sum(total, keepdims=True)
    factor_ref[...] = jnp.broadcast_to(CLIP / jnp.sqrt(total / ENTRIES + EPS), (8, 128))

    values = []
    for cc in range(2):
        v = jnp.concatenate([b3[zz, cc, 0, pl.ds(z, 1), :] for zz in range(NZ)], axis=0)
        shifted = jnp.concatenate([v[:, 8:], v[:, :8]], axis=1)
        values.append(jnp.where(c == 0, v, shifted))
    sums = [zero8] * 8
    for m in range(8):
        for cc in range(2):
            at = (m * 2 + cc) * 8
            rk = rk_s[at : at + 8, :]
            val = zero8
            for r in range(8):
                col = jnp.broadcast_to(values[cc][:, m * 16 + r : m * 16 + r + 1], (8, TOK))
                val += jnp.where(rk == float(r), col, 0.0)
            expert = ((2 * (m % 4) + cc) * 16 + m // 4 + 2 * row8).astype(F32)
            for kk in range(8):
                sums[kk] += jnp.where(own[kk : kk + 1, :] == expert, val, 0.0)
    router_ref[...] = jnp.concatenate([jnp.sum(s, axis=0, keepdims=True) for s in sums], axis=0)

    for cp in meta_copies + zmeta + packs + pre + e3:
        cp.wait_send()
    for h in range(2):
        for part in range(2):
            for cp in own_zsends(h, part):
                cp.wait_send()
            for k in range(NZ):
                sib_copy(step_z(z, k), k, h, part).wait_send()
                if 1 <= k <= 4 or (k == 5 and h == 0) or (k == 6 and h == 1):
                    zsend(
                        step_z(z, k), h, part, zr_s.at[k, h, part], zr_r.at[7, h, part], 1
                    ).wait_send()
    for j in range(STEPS - NB, STEPS):
        fh_sent(j)
    for j in range(STEPS):
        fw_copy(j).wait_send()
    for m in range(8):
        @pl.when(m != me8)
        def _(m=m):
            gv_copy(m).wait_send()
    for j in range(16):
        @pl.when(j != me16)
        def _(j=j):
            e1_copy(j).wait_send()
    hg_copy.wait()
    for h in range(2):
        wg_copy(h).wait()


BLOCKS = 8
BR = FFH // BLOCKS


def finish(wg_hbm, hg_hbm, router_in, factor_ref, out_hbm, hg_out, router_out, wide, narrow, hidden, sems, out_sems, hg_sem):
    hg_in = pltpu.make_async_copy(hg_hbm, hidden, hg_sem.at[0])
    hg_copy = pltpu.make_async_copy(hidden, hg_out, hg_sem.at[1])
    loads = [
        pltpu.make_async_copy(wg_hbm.at[pl.ds(j * BR, BR)], wide.at[j], sems.at[j]) for j in range(BLOCKS)
    ]
    stores = [
        pltpu.make_async_copy(narrow.at[j], out_hbm.at[pl.ds(j * BR, BR)], out_sems.at[j]) for j in range(BLOCKS)
    ]
    loads[0].start()
    hg_in.start()
    for cp in loads[1:]:
        cp.start()
    router_out[...] = router_in[...]
    factor = factor_ref[0:1, 0:1]
    for j in range(BLOCKS):
        loads[j].wait()
        narrow[j] = (wide[j] * factor).astype(BF16)
        stores[j].start()
        if j == 0:
            hg_in.wait()
            hg_copy.start()
    for cp in stores:
        cp.wait()
    hg_copy.wait()


def per_device(grad_out, expert_ids, gate_probs, down_weight, hidden_act):
    anywhere = pl.BlockSpec(memory_space=pl.ANY)
    vmem = pl.BlockSpec(memory_space=pltpu.VMEM)
    dma = pltpu.SemaphoreType.DMA
    small = pltpu.VMEM((2, 8, 128), F32)
    weight_grad, hidden, router, factor = pl.pallas_call(
        kernel,
        out_shape=(
            jax.ShapeDtypeStruct((FFH, D), F32),
            jax.ShapeDtypeStruct((SLOTS, FFH), BF16),
            jax.ShapeDtypeStruct((8, TOK), F32),
            jax.ShapeDtypeStruct((8, 128), F32),
        ),
        in_specs=[anywhere, vmem, vmem, anywhere, anywhere],
        out_specs=(anywhere, anywhere, vmem, vmem),
        scratch_shapes=[
            pltpu.VMEM((NZ, 2, 2 * TOK, TW), BF16),
            pltpu.VMEM((NZ, 256, D), BF16),
            pltpu.VMEM((NB, 128, TW), BF16),
            pltpu.VMEM((FFH, D), BF16),
            pltpu.VMEM((SLOTS, FFH), BF16),
            pltpu.VMEM((SLOTS, FFH), BF16),
            pltpu.VMEM((FFH, D), F32),
            pltpu.VMEM((NZ, 2, 128, 256), BF16),
            pltpu.VMEM((4, 16, 128), BF16),
            pltpu.VMEM((4, NZ, 16, 128), BF16),
            small,
            pltpu.VMEM((8, 2, 8, 128), F32),
            pltpu.VMEM((2, 256, FFH), F32),
            pltpu.VMEM((2, FFH, 256), BF16),
            pltpu.VMEM((2, 256, 128), F32),
            pltpu.VMEM((128, 128), F32),
            pltpu.VMEM((8, 128), F32),
            small,
            pltpu.VMEM((16, 2, 8, 128), F32),
            pltpu.VMEM((16, 2, 8, 128), F32),
            small,
            pltpu.VMEM((NZ, 2, 2, 8, 128), F32),
            dma((4,)),
            dma((3,)),
            dma((3,)),
            dma((3,)),
            dma((NZ,)),
            dma((NZ,)),
            dma((3,)),
            dma((3,)),
            dma((2,)),
            dma((2,)),
            dma((NZ, 2, 2)),
            dma((NZ, 2, 2)),
            dma((NZ, 2, 2)),
            dma((NZ, 2, 2)),
            dma((NB,)),
            dma((STEPS, 2)),
            dma((NB, 2)),
            dma((STEPS,)),
            dma((STEPS,)),
            dma((8,)),
            dma((8,)),
            dma((16,)),
            dma((16,)),
            dma((NZ, 2)),
            dma((NZ, 2)),
        ],
        compiler_params=pltpu.CompilerParams(
            collective_id=0, has_side_effects=True, vmem_limit_bytes=60 * 2**20
        ),
    )(grad_out, expert_ids.T, gate_probs.T, down_weight, hidden_act)
    clipped, hidden_grad, router = pl.pallas_call(
        finish,
        out_shape=(
            jax.ShapeDtypeStruct((FFH, D), BF16),
            jax.ShapeDtypeStruct((SLOTS, FFH), BF16),
            jax.ShapeDtypeStruct((8, TOK), F32),
        ),
        in_specs=[anywhere, anywhere, vmem, vmem],
        out_specs=(anywhere, anywhere, vmem),
        scratch_shapes=[
            pltpu.VMEM((BLOCKS, BR, D), F32),
            pltpu.VMEM((BLOCKS, BR, D), BF16),
            pltpu.VMEM((SLOTS, FFH), BF16),
            dma((BLOCKS,)),
            dma((BLOCKS,)),
            dma((2,)),
        ],
        compiler_params=pltpu.CompilerParams(vmem_limit_bytes=60 * 2**20),
    )(weight_grad, hidden, router, factor)
    return clipped, hidden_grad, router.T


def solution(mesh):
    both = ("node", "local")
    return jax.shard_map(
        per_device,
        mesh=mesh,
        in_specs=(P(both, None), P(both, None), P(both, None), P(both, None), P(None, both)),
        out_specs=(P(both, None), P(None, both), P(both, None)),
        check_vma=False,
    )
```

```python
import jax
import jax.numpy as jnp
from jax import lax
from jax.experimental import pallas as pl
from jax.experimental.pallas import tpu as pltpu
from jax.sharding import PartitionSpec as P

MESH = pl.DeviceIdType.MESH
F32 = jnp.float32
BF16 = jnp.bfloat16

D = 3584
FFH = 512
TOK = 128
SLOTS = 2048
ENTRIES = 469762048
CLIP = 0.25
EPS = 1e-06

DH = D // 2
GH = 640
AH = DH - GH
TW = DH + GH
NB = 6
NZ = 8
STEPS = 2 * NZ
PIECES = ((0, AH), (AH, GH), (DH, GH))
WAITS = ((0, AH), (AH, TW - AH))
LF = 2
LC = 4


def nt(a, b):
    return lax.dot_general(a, b, (((1,), (1,)), ((), ())), preferred_element_type=F32)


def step_z(z, k):
    return lax.rem(z + ((k + 1) // 2) * (1 - 2 * lax.rem(k, 2)) + NZ, NZ)


def step_kh(j):
    g, u = (j + 2) // 4, lax.rem(j + 2, 4)
    mid = (g + 3) // 4 - g // 4
    h = mid * (u // 2) + (1 - mid) * lax.rem(u, 2)
    side = mid * lax.rem(u, 2)
    return mid * (2 * g - 1 + side) + (g // 4) * 7, h, side


def tiles(width):
    out, at = [], 0
    while at < width:
        size = min(256, width - at)
        out.append((at, size))
        at += size
    return out


def kernel(
    tok_hbm, ids_ref, gate_ref, w_hbm, act_hbm,
    wg_hbm, hg_hbm, router_ref, factor_ref,
    tx, rows, stage, wv, actv, hgv, wg, sel, meta, metaz, gvb, gvr, proj, sct, gate_s, rk_s, sq_s,
    pv, a1, b1, a3, b3,
    in_sem, out_sem, meta_s, meta_r, zmeta_s, zmeta_r, pack_s, pack_r, pc_s, pc_r, zr_s, zr_r, sib_s, sib_r,
    fh_s, fh_r, fh_l, fw_s, fw_r, gv_s, gv_r, e1_s, e1_r, e3_s, e3_r,
):
    node = lax.axis_index("node")
    local = lax.axis_index("local")
    y, c = node // 2, lax.rem(node, 2)
    z, x = local // 4, lax.rem(local, 4)
    xp = lax.rem(x, 2)
    pair = x // 2
    qx = lax.rem(xp + pair, 2)
    x_partner = x + 1 - 2 * xp
    me8 = pair * 4 + y
    me16 = x * 4 + y

    def dev(xx, yy, zz, cc):
        return (2 * yy + cc, 4 * zz + xx)

    partner = dev(x_partner, y, z, c)
    sibling = dev(x, y, z, 1 - c)
    diagonal = dev(x_partner, y, z, 1 - c)

    def entry_x(p):
        return qx + p * (3 - 2 * qx)

    def remote(src, dst, ss, rs, to):
        return pltpu.make_async_remote_copy(
            src_ref=src, dst_ref=dst, send_sem=ss, recv_sem=rs, device_id=to, device_id_type=MESH
        )

    def landed(dst, rs):
        pltpu.make_async_copy(dst, dst, rs).wait()

    def zpeer(d, cc=None):
        return dev(x, y, lax.rem(z + d + NZ, NZ), c if cc is None else cc)

    own_rows = pl.ds(pl.multiple_of(c * TOK, TOK), TOK)
    sib_rows = pl.ds(pl.multiple_of((1 - c) * TOK, TOK), TOK)
    tok_copies = [
        pltpu.make_async_copy(
            tok_hbm.at[:, pl.ds(h * DH, DH)], tx.at[z, h, own_rows, pl.ds(0, DH)], in_sem.at[h]
        )
        for h in range(2)
    ]
    for cp in tok_copies:
        cp.start()
    act_copy = pltpu.make_async_copy(act_hbm, actv, in_sem.at[2])
    w_copy = pltpu.make_async_copy(w_hbm, wv, in_sem.at[3])
    act_copy.start()
    w_copy.start()
    mine = xp * 2 + c
    routing = jnp.concatenate([ids_ref[...].astype(F32), gate_ref[...].astype(F32)], axis=0).astype(BF16)
    meta[mine] = routing
    metaz[mine, z] = routing

    barrier = pltpu.get_barrier_semaphore()

    def greet(to):
        pl.semaphore_signal(barrier, inc=1, device_id=to, device_id_type=MESH)

    for j in range(16):
        @pl.when(j != me16)
        def _(j=j):
            greet(dev(j // 4, j % 4, z, c))
    greet(sibling)
    greet(diagonal)
    for d in range(1, NZ):
        greet(zpeer(d))
        greet(zpeer(d, 1 - c))
    pl.semaphore_wait(barrier, 15 + 2 + 14)

    others = ((partner, (1 - xp) * 2 + c), (sibling, xp * 2 + 1 - c), (diagonal, (1 - xp) * 2 + 1 - c))
    meta_copies = [
        remote(meta.at[mine], meta.at[mine], meta_s.at[j], meta_r.at[j], to)
        for j, (to, _) in enumerate(others)
    ]
    zmeta = [
        remote(metaz.at[mine, z], metaz.at[mine, z], zmeta_s.at[d], zmeta_r.at[d], zpeer(d))
        for d in range(1, NZ)
    ]
    packs = [
        remote(metaz.at[mine], metaz.at[mine], pack_s.at[j], pack_r.at[j], to)
        for j, (to, _) in enumerate(others)
    ]
    for cp in meta_copies + zmeta:
        cp.start()
    part_cols = (pl.ds(0, DH), pl.ds(DH, GH))
    pre = [
        remote(
            tx.at[z, h, own_rows, pl.ds(AH, GH)], tx.at[z, h, own_rows, pl.ds(DH, GH)],
            pc_s.at[h], pc_r.at[h], partner,
        )
        for h in range(2)
    ]

    def zsend(zs, h, part, ss, rs, d):
        ref = tx.at[zs, h, own_rows, part_cols[part]]
        return remote(ref, ref, ss, rs, zpeer(d))

    def sib_copy(zs, k, h, part):
        ref = tx.at[zs, h, own_rows, part_cols[part]]
        return remote(ref, ref, sib_s.at[k, h, part], sib_r.at[k, h, part], sibling)

    def own_zsends(h, part):
        return (
            zsend(z, h, part, zr_s.at[0, h, part], zr_r.at[1, h, part], 1),
            zsend(z, h, part, zr_s.at[7, h, part], zr_r.at[2, h, part], -1),
        )

    for h in range(2):
        tok_copies[h].wait()
        pre[h].start()
        sib_copy(z, 0, h, 0).start()
        if h == 0:
            for cp in own_zsends(0, 0):
                cp.start()

    row8 = lax.broadcasted_iota(jnp.int32, (8, TOK), 0)
    before = jnp.where(
        lax.broadcasted_iota(jnp.int32, (TOK, TOK), 0) < lax.broadcasted_iota(jnp.int32, (TOK, TOK), 1),
        1.0, 0.0,
    ).astype(BF16)
    expert8 = ((2 * lax.rem(row8, 4) + c) * 16 + 2 * z + row8 // 4).astype(F32)
    rank8 = row8.astype(F32)
    zero8 = jnp.zeros((8, TOK), F32)

    def build_from(data, k):
        zs = step_z(z, k)
        for s in range(2):
            hits, gates = [], []
            for cs in range(2):
                one = data(lax.rem(xp + s, 2) * 2 + cs, zs).astype(F32)
                hit_sum, gate_sum = zero8, zero8
                for kk in range(8):
                    hit = one[kk : kk + 1, :] == expert8
                    hit_sum += jnp.where(hit, 1.0, 0.0)
                    gate_sum += jnp.where(hit, one[8 + kk : 9 + kk, :], 0.0)
                hits.append(hit_sum)
                gates.append(gate_sum)
            hit16 = jnp.concatenate(hits, axis=0)
            rank = jnp.dot(hit16.astype(BF16), before, preferred_element_type=F32)
            rank = jnp.where(hit16 > 0.5, rank, -1.0)
            picks, gate_picks = [], []
            for m in range(8):
                for cs in range(2):
                    at = rank[cs * 8 + m : cs * 8 + m + 1, :] == rank8
                    pick = jnp.where(at, 1.0, 0.0)
                    gate_pick = jnp.where(at, gates[cs][m : m + 1, :], 0.0)
                    pair_of = (lambda t: [t, zero8]) if cs == 0 else (lambda t: [zero8, t])
                    picks.append(jnp.concatenate(pair_of(pick), axis=1))
                    gate_picks.append(jnp.concatenate(pair_of(gate_pick), axis=1))
            sel[k, s] = jnp.concatenate(picks, axis=0).astype(BF16)
            weighted = jnp.concatenate(gate_picks, axis=0).astype(BF16)
            gate_row = nt(jnp.ones((16, 2 * TOK), BF16), weighted)
            gvb[s, pl.ds(zs, 1), :] = gate_row[0:1]

    def build(k, carry):
        build_from(lambda who, zs: metaz[who, zs], k)
        return carry

    def gv_copy(m):
        return remote(
            gvb, gvr.at[me8], gv_s.at[m], gv_r.at[me8], dev(entry_x(m // 4), m % 4, z, c)
        )

    def z_arrive(k, h, part):
        zs = step_z(z, k)
        landed(tx.at[zs, h, own_rows, part_cols[part]], zr_r.at[k, h, part])
        odd = lax.rem(k, 2)
        onward = (k <= 4) | ((k == 5) & (h == 0)) | ((k == 6) & (h == 1))
        to_k = k + 2 - k // 6

        @pl.when(onward & (odd == 1))
        def _():
            zsend(zs, h, part, zr_s.at[k, h, part], zr_r.at[to_k, h, part], 1).start()

        @pl.when(onward & (odd == 0))
        def _():
            zsend(zs, h, part, zr_s.at[k, h, part], zr_r.at[to_k, h, part], -1).start()

        sib_copy(zs, k, h, part).start()

    def row_of(q, i, ys):
        return pl.multiple_of(((q * 2 + i) * 4 + ys) * 16, 16)

    def half(h, at, width):
        return pl.ds(pl.multiple_of(h * DH + at, 128), width)

    def fh_pair(j, m, part):
        k, h, _ = step_kh(j)
        zs = step_z(z, k)
        b = lax.rem(j, NB)
        start, width = PIECES[part]
        src = stage.at[b, pl.ds(pl.multiple_of(m * 16, 16), 16), pl.ds(start, width)]
        source = 1 - qx if part == 2 else qx
        return src, rows.at[zs, pl.ds(row_of(source, pair, y), 16), half(h, min(start, AH), width)]

    def fh_start(j, parts):
        b = lax.rem(j, NB)
        for part in parts:
            for far, dy in ((1, 2), (0, 2), (1, 1), (1, 3), (0, 1), (0, 3), (1, 0), (0, 0)):
                yy = lax.rem(y + dy, 4)
                m = (pair + far - 2 * far * pair) * 4 + yy
                src, dst = fh_pair(j, m, part)
                if far or dy:
                    xx = x + far * (3 - 2 * x)
                    remote(src, dst, fh_s.at[b], fh_r.at[j, min(part, 1)], dev(xx, yy, z, c)).start()
                else:
                    pltpu.make_async_copy(src, dst, fh_l.at[b, min(part, 1)]).start()

    def fh_sent(j):
        b = lax.rem(j, NB)
        landed(stage.at[b, pl.ds(0, 112)], fh_s.at[b])

    def fh_landed(j, group):
        b = lax.rem(j, NB)
        cols = pl.ds(*WAITS[group])
        landed(stage.at[b, pl.ds(0, 112), cols], fh_r.at[j, group])
        landed(stage.at[b, pl.ds(0, 16), cols], fh_l.at[b, group])

    def fw_copy(j):
        k, h, _ = step_kh(j)
        ref = rows.at[step_z(z, k), pl.ds(pl.multiple_of(qx * 128, 128), 128), half(h, 0, AH)]
        return remote(ref, ref, fw_s.at[j], fw_r.at[j], partner)

    def gather(j, parts):
        k, h, _ = step_kh(j)
        zs = step_z(z, k)
        b = lax.rem(j, NB)
        for s in parts:
            start, width = ((0, DH), (DH, GH))[s]
            pick = sel[k, s]
            for at, size in tiles(width):
                cols = pl.ds(start + at, size)
                picked = jnp.dot(pick, tx[zs, h, :, cols], preferred_element_type=F32)
                stage[b, :, cols] = picked.astype(BF16)

    def acts(zs, cols):
        blocks = [
            actv[pl.ds(pl.multiple_of(ns * 256 + zs * 32, 32), 32), cols].astype(F32) for ns in range(8)
        ]
        pieces = []
        for q in range(2):
            for i in range(2):
                xs = q + i * (3 - 2 * q)
                for ns in range(8):
                    pieces.append(blocks[ns][xs * 8 : xs * 8 + 8])
        return jnp.concatenate(pieces, axis=0)

    def chunk(j):
        k, h, _ = step_kh(j)
        zs = step_z(z, k)
        slot = lax.rem(k, 2)

        @pl.when(h == 0)
        def _():
            lane = lax.broadcasted_iota(jnp.int32, (256, 128), 1)
            row = lax.broadcasted_iota(jnp.int32, (256, 128), 0)
            mine16 = lane == me8 * 16 + lax.rem(row, 16)
            gate_rows = []
            for q in range(2):
                for i in range(8):
                    one = gvr[i, lax.rem(qx + q, 2), pl.ds(zs, 1), :]
                    gate_rows.append(jnp.broadcast_to(one, (16, 128)))
            picked = jnp.where(mine16, jnp.concatenate(gate_rows, axis=0), 0.0).astype(BF16)
            gate = jnp.dot(picked, jnp.ones((128, 128), BF16), preferred_element_type=F32)
            gate_s[slot] = gate
            for ct in range(4):
                cols = pl.ds(ct * 128, 128)
                sct[slot, ct * 128 : ct * 128 + 128, :] = jnp.transpose(gate * acts(zs, cols)).astype(BF16)
            proj[slot] = jnp.zeros((256, FFH), F32)

        proj[slot] += nt(rows[zs, :, half(h, 0, DH)], wv[:, half(h, 0, DH)])

        @pl.when(h == 1)
        def _():
            total = jnp.zeros((256, 128), F32)
            for ct in range(4):
                cols = pl.ds(ct * 128, 128)
                pr = proj[slot, :, cols]
                total += acts(zs, cols) * pr
                hidden = gate_s[slot] * pr
                for ns in range(8):
                    back = []
                    for xs in range(4):
                        at = ((((xs % 2) + (xs // 2)) % 2 * 2 + xs // 2) * 8 + ns) * 8
                        back.append(hidden[at : at + 8])
                    hgv[pl.ds(pl.multiple_of(ns * 256 + zs * 32, 32), 32), cols] = jnp.concatenate(
                        back, axis=0
                    ).astype(BF16)
            ones = jnp.ones((16, 128), BF16)
            hi = total.astype(BF16)
            rest = total - hi.astype(F32)
            mid = rest.astype(BF16)
            low = (rest - mid.astype(F32)).astype(BF16)
            sums = nt(ones, hi) + nt(ones, mid) + nt(ones, low)
            for q in range(2):
                pv[q, pl.ds(zs, 1), :] = sums[0:1, q * 128 : q * 128 + 128]

        for at, size in tiles(DH):
            cols = half(h, at, size)
            wg[:, cols] += jnp.dot(sct[slot], rows[zs, :, cols], preferred_element_type=F32)

    def square(at):
        acc = zero8
        for start, size in tiles(DH):
            w = wg[:, at + start : at + start + size]
            s = jnp.sum((w * w).reshape(FFH // 8, 8, size), axis=0)
            acc += s[:, :128] + s[:, 128:]
        return acc

    def wg_copy(h):
        cols = pl.ds(h * DH, DH)
        return pltpu.make_async_copy(wg.at[:, cols], wg_hbm.at[:, cols], out_sem.at[h])

    def body(j, carry):
        @pl.when(j < STEPS)
        def _():
            k, h, side = step_kh(j)
            zs = step_z(z, k)

            @pl.when(j >= NB)
            def _():
                fh_sent(j - NB)

            for part in range(2):
                @pl.when((k > 0) & (side == 0))
                def _(part=part):
                    z_arrive(k, h, part)

                    @pl.when(k < 7)
                    def _():
                        z_arrive(k + 1, h, part)

                landed(tx.at[zs, h, sib_rows, part_cols[part]], sib_r.at[k, h, part])
                gather(j, (part,))
                fh_start(j, (0, 1) if part == 0 else (2,))

        @pl.when(j == 1)
        def _():
            for d in range(1, NZ):
                landed(metaz.at[mine, lax.rem(z - d + NZ, NZ)], zmeta_r.at[d])
            for cp in packs:
                cp.start()

        @pl.when((j >= LF) & (j < STEPS + LF))
        def _():
            fh_landed(j - LF, 0)
            fw_copy(j - LF).start()

        @pl.when(j == 1)
        def _():
            for i, (_, slot) in enumerate(others):
                landed(metaz.at[slot], pack_r.at[i])
            lax.fori_loop(1, NZ, build, 0)
            gvr[me8] = gvb[...]
            for m in range(8):
                @pl.when(m != me8)
                def _(m=m):
                    gv_copy(m).start()
            wg[...] = jnp.zeros((FFH, D), F32)

        @pl.when(j == LC)
        def _():
            act_copy.wait()
            w_copy.wait()
            for i in range(8):
                @pl.when(i != me8)
                def _(i=i):
                    landed(gvr.at[i], gv_r.at[i])

        @pl.when(j >= LC)
        def _():
            k, h, _ = step_kh(j - LC)
            other = pl.ds(pl.multiple_of((1 - qx) * 128, 128), 128)
            landed(rows.at[step_z(z, k), other, half(h, 0, AH)], fw_r.at[j - LC])
            fh_landed(j - LC, 1)
            chunk(j - LC)

        @pl.when(j == STEPS + LC - 2)
        def _():
            sq_s[...] = square(0)
            wg_copy(0).start()

        return carry

    for j, (_, slot) in enumerate(others):
        landed(meta.at[slot], meta_r.at[j])
    build_from(lambda who, zs: meta[who], 0)
    for part in range(2):
        if part == 1:
            pre[0].wait_recv()
            for cp in own_zsends(0, 1):
                cp.start()
            sib_copy(z, 0, 0, 1).start()
            for cp in own_zsends(1, 0):
                cp.start()
        landed(tx.at[z, 0, sib_rows, part_cols[part]], sib_r.at[0, 0, part])
        gather(0, (part,))
        fh_start(0, (0, 1) if part == 0 else (2,))
    pre[1].wait_recv()
    for cp in own_zsends(1, 1):
        cp.start()
    sib_copy(z, 0, 1, 1).start()
    lax.fori_loop(1, STEPS + LC, body, 0)

    hg_copy = pltpu.make_async_copy(hgv, hg_hbm, out_sem.at[2])
    wg_copy(1).start()
    hg_copy.start()

    squares = sq_s[...] + square(DH)
    for j in range(16):
        xx, yy = j // 4, j % 4
        back = pv[(xx % 2 + xx // 2) % 2]
        lanes = (xx // 2 * 4 + yy) * 16
        a1[j, 0] = jnp.concatenate([back[:, lanes : lanes + 16], jnp.zeros((8, 112), F32)], axis=1)
        a1[j, 1] = squares

    def e1_copy(j):
        return remote(a1.at[j], b1.at[me16], e1_s.at[j], e1_r.at[me16], dev(j // 4, j % 4, z, c))

    for j in range(16):
        @pl.when(j != me16)
        def _(j=j):
            e1_copy(j).start()
    b1[me16] = a1[me16]

    own = meta[mine].astype(F32)
    ranks = []
    for m in range(8):
        for cc in range(2):
            expert = ((2 * (m % 4) + cc) * 16 + m // 4 + 2 * row8).astype(F32)
            hit_sum = zero8
            for kk in range(8):
                hit_sum += jnp.where(own[kk : kk + 1, :] == expert, 1.0, 0.0)
            ranks.append(hit_sum)
    hit128 = jnp.concatenate(ranks, axis=0)
    rank = jnp.dot(hit128.astype(BF16), before, preferred_element_type=F32)
    rk_s[...] = jnp.where(hit128 > 0.5, rank, -1.0)

    for j in range(16):
        @pl.when(j != me16)
        def _(j=j):
            landed(b1.at[j], e1_r.at[j])
    a3[0] = jnp.concatenate(
        [
            b1[2 * p * 4 + yy, 0][:, 0:16] + b1[(2 * p + 1) * 4 + yy, 0][:, 0:16]
            for p in range(2)
            for yy in range(4)
        ],
        axis=1,
    )
    total = b1[0, 1]
    for j in range(1, 16):
        total += b1[j, 1]
    a3[1] = total

    def e3_copy(d, cc):
        to_c = c if cc == 0 else 1 - c
        return remote(
            a3, b3.at[z, c], e3_s.at[d, cc], e3_r.at[d, cc], zpeer(d, to_c)
        )

    e3 = [e3_copy(d, cc) for d in range(NZ) for cc in range(2) if d or cc]
    for cp in e3:
        cp.start()
    b3[z, c] = a3[...]
    for d in range(NZ):
        for cc in range(2):
            if d or cc:
                from_c = c if cc == 0 else 1 - c
                landed(b3.at[lax.rem(z - d + NZ, NZ), from_c], e3_r.at[d, cc])
    total = zero8
    for zz in range(NZ):
        for cc in range(2):
            total += b3[zz, cc, 1]
    total = jnp.sum(total, keepdims=True)
    factor_ref[...] = jnp.broadcast_to(CLIP / jnp.sqrt(total / ENTRIES + EPS), (8, 128))

    values = []
    for cc in range(2):
        v = jnp.concatenate([b3[zz, cc, 0, pl.ds(z, 1), :] for zz in range(NZ)], axis=0)
        shifted = jnp.concatenate([v[:, 8:], v[:, :8]], axis=1)
        values.append(jnp.where(c == 0, v, shifted))
    sums = [zero8] * 8
    for m in range(8):
        for cc in range(2):
            at = (m * 2 + cc) * 8
            rk = rk_s[at : at + 8, :]
            val = zero8
            for r in range(8):
                col = jnp.broadcast_to(values[cc][:, m * 16 + r : m * 16 + r + 1], (8, TOK))
                val += jnp.where(rk == float(r), col, 0.0)
            expert = ((2 * (m % 4) + cc) * 16 + m // 4 + 2 * row8).astype(F32)
            for kk in range(8):
                sums[kk] += jnp.where(own[kk : kk + 1, :] == expert, val, 0.0)
    router_ref[...] = jnp.concatenate([jnp.sum(s, axis=0, keepdims=True) for s in sums], axis=0)

    for cp in meta_copies + zmeta + packs + pre + e3:
        cp.wait_send()
    for h in range(2):
        for part in range(2):
            for cp in own_zsends(h, part):
                cp.wait_send()
            for k in range(NZ):
                sib_copy(step_z(z, k), k, h, part).wait_send()
                if 1 <= k <= 4 or (k == 5 and h == 0) or (k == 6 and h == 1):
                    zsend(
                        step_z(z, k), h, part, zr_s.at[k, h, part], zr_r.at[7, h, part], 1
                    ).wait_send()
    for j in range(STEPS - NB, STEPS):
        fh_sent(j)
    for j in range(STEPS):
        fw_copy(j).wait_send()
    for m in range(8):
        @pl.when(m != me8)
        def _(m=m):
            gv_copy(m).wait_send()
    for j in range(16):
        @pl.when(j != me16)
        def _(j=j):
            e1_copy(j).wait_send()
    hg_copy.wait()
    for h in range(2):
        wg_copy(h).wait()


BLOCKS = 8
BR = FFH // BLOCKS


def finish(wg_hbm, hg_hbm, router_in, factor_ref, out_hbm, hg_out, router_out, wide, narrow, hidden, sems, out_sems, hg_sem):
    hg_in = pltpu.make_async_copy(hg_hbm, hidden, hg_sem.at[0])
    hg_copy = pltpu.make_async_copy(hidden, hg_out, hg_sem.at[1])
    loads = [
        pltpu.make_async_copy(wg_hbm.at[pl.ds(j * BR, BR)], wide.at[j], sems.at[j]) for j in range(BLOCKS)
    ]
    stores = [
        pltpu.make_async_copy(narrow.at[j], out_hbm.at[pl.ds(j * BR, BR)], out_sems.at[j]) for j in range(BLOCKS)
    ]
    loads[0].start()
    hg_in.start()
    for cp in loads[1:]:
        cp.start()
    router_out[...] = router_in[...]
    factor = factor_ref[0:1, 0:1]
    for j in range(BLOCKS):
        loads[j].wait()
        narrow[j] = (wide[j] * factor).astype(BF16)
        stores[j].start()
        if j == 0:
            hg_in.wait()
            hg_copy.start()
    for cp in stores:
        cp.wait()
    hg_copy.wait()


def per_device(grad_out, expert_ids, gate_probs, down_weight, hidden_act):
    anywhere = pl.BlockSpec(memory_space=pl.ANY)
    vmem = pl.BlockSpec(memory_space=pltpu.VMEM)
    dma = pltpu.SemaphoreType.DMA
    small = pltpu.VMEM((2, 8, 128), F32)
    weight_grad, hidden, router, factor = pl.pallas_call(
        kernel,
        out_shape=(
            jax.ShapeDtypeStruct((FFH, D), F32),
            jax.ShapeDtypeStruct((SLOTS, FFH), BF16),
            jax.ShapeDtypeStruct((8, TOK), F32),
            jax.ShapeDtypeStruct((8, 128), F32),
        ),
        in_specs=[anywhere, vmem, vmem, anywhere, anywhere],
        out_specs=(anywhere, anywhere, vmem, vmem),
        scratch_shapes=[
            pltpu.VMEM((NZ, 2, 2 * TOK, TW), BF16),
            pltpu.VMEM((NZ, 256, D), BF16),
            pltpu.VMEM((NB, 128, TW), BF16),
            pltpu.VMEM((FFH, D), BF16),
            pltpu.VMEM((SLOTS, FFH), BF16),
            pltpu.VMEM((SLOTS, FFH), BF16),
            pltpu.VMEM((FFH, D), F32),
            pltpu.VMEM((NZ, 2, 128, 256), BF16),
            pltpu.VMEM((4, 16, 128), BF16),
            pltpu.VMEM((4, NZ, 16, 128), BF16),
            small,
            pltpu.VMEM((8, 2, 8, 128), F32),
            pltpu.VMEM((2, 256, FFH), F32),
            pltpu.VMEM((2, FFH, 256), BF16),
            pltpu.VMEM((2, 256, 128), F32),
            pltpu.VMEM((128, 128), F32),
            pltpu.VMEM((8, 128), F32),
            small,
            pltpu.VMEM((16, 2, 8, 128), F32),
            pltpu.VMEM((16, 2, 8, 128), F32),
            small,
            pltpu.VMEM((NZ, 2, 2, 8, 128), F32),
            dma((4,)),
            dma((3,)),
            dma((3,)),
            dma((3,)),
            dma((NZ,)),
            dma((NZ,)),
            dma((3,)),
            dma((3,)),
            dma((2,)),
            dma((2,)),
            dma((NZ, 2, 2)),
            dma((NZ, 2, 2)),
            dma((NZ, 2, 2)),
            dma((NZ, 2, 2)),
            dma((NB,)),
            dma((STEPS, 2)),
            dma((NB, 2)),
            dma((STEPS,)),
            dma((STEPS,)),
            dma((8,)),
            dma((8,)),
            dma((16,)),
            dma((16,)),
            dma((NZ, 2)),
            dma((NZ, 2)),
        ],
        compiler_params=pltpu.CompilerParams(
            collective_id=0, has_side_effects=True, vmem_limit_bytes=60 * 2**20
        ),
    )(grad_out, expert_ids.T, gate_probs.T, down_weight, hidden_act)
    clipped, hidden_grad, router = pl.pallas_call(
        finish,
        out_shape=(
            jax.ShapeDtypeStruct((FFH, D), BF16),
            jax.ShapeDtypeStruct((SLOTS, FFH), BF16),
            jax.ShapeDtypeStruct((8, TOK), F32),
        ),
        in_specs=[anywhere, anywhere, vmem, vmem],
        out_specs=(anywhere, anywhere, vmem),
        scratch_shapes=[
            pltpu.VMEM((BLOCKS, BR, D), F32),
            pltpu.VMEM((BLOCKS, BR, D), BF16),
            pltpu.VMEM((SLOTS, FFH), BF16),
            dma((BLOCKS,)),
            dma((BLOCKS,)),
            dma((2,)),
        ],
        compiler_params=pltpu.CompilerParams(vmem_limit_bytes=60 * 2**20),
    )(weight_grad, hidden, router, factor)
    return clipped, hidden_grad, router.T


def solution(mesh):
    both = ("node", "local")
    return jax.shard_map(
        per_device,
        mesh=mesh,
        in_specs=(P(both, None), P(both, None), P(both, None), P(both, None), P(None, both)),
        out_specs=(P(both, None), P(None, both), P(both, None)),
        check_vma=False,
    )
```
